512 devices in a mesh: ep: 32 (over z, core), rep: 16 (over y, x).
Axes of the slice: x: 4, y: 4, z: 16, core: 2. Of those that a mesh axis runs over, the one named last changes fastest.
Arguments:
- frames: bfloat16 [65536, 1024], P(('ep', 'rep')), may hold values from -6 to 6
- lengths: int32 [512], P(('ep', 'rep')), may hold values from 64 to 128
- routes: int32 [65536, 2], P(('ep', 'rep')), may hold values from 0 to 31, all different within a row; in each aligned block of 128 rows (0 to 127, 128 to 255, ...) at most 8 rows name the same one
- gate_weights: float32 [65536, 2], P(('ep', 'rep')), may hold values from 0.25 to 1
- kernel: float32 [31, 1024], replicated, may hold values from -1 to 1
- up_weight: bfloat16 [32, 2048, 1024], P('ep', 'rep'), may hold values from -0.1875 to 0.1875
- down_weight: bfloat16 [32, 2048, 1024], P('ep', 'rep'), may hold values from -0.125 to 0.125
- cotangent: bfloat16 [65536, 1024], P(('ep', 'rep')), may hold values from -1.5 to 1.5
Outputs:
- block_out: bfloat16 [65536, 1024], P(('ep', 'rep'))
- frame_grad: bfloat16 [65536, 1024], P(('ep', 'rep'))
- up_grad: float32 [32, 2048, 1024], P('ep', 'rep')
- down_grad: float32 [32, 2048, 1024], P('ep', 'rep')
The draws below stay inside these ranges and needn't reach their ends.
Inputs may be any that keep to these rules, and one draw needn't show every extreme that they name: The 128 frames of one utterance name every expert in exactly 8 of their routes; a frame's 2 experts differ.
All inputs are finite; a program needn't handle non-finite values.
Results may differ from the reference program's by a relative error of at most 0.015.
Values may be sent and summed in bfloat16 or wider, within the bound.
A program may use at most 128 MiB of HBM per device.

```python
import math
import jax
import jax.numpy as jnp
import numpy as np
from jax import lax

D = 1024
W = 2048
KW = 31
TOP = 2
TOK_DEV = 128
EXPERTS = 32
CAP = 8
UTTS = 512
FRAMES = 65536
N_EP = 32
N_REP = 16


def draw_lengths(key, part):
    key = jax.random.fold_in(key, 11)
    values = jax.random.randint(key, (UTTS,), TOK_DEV // 2, TOK_DEV + 1).astype(jnp.int32)
    values = values.at[0].set(TOK_DEV)
    return values.at[1].set(TOK_DEV // 2)


def levels(rng, dims, shards, smallest, largest):
    factor_of = 1.0
    for position, parts in shards:
        steps = jax.random.uniform(jax.random.fold_in(jax.random.fold_in(rng, 6), position), (parts,), jnp.float32, smallest / len(shards), largest / len(shards))
        factor_of = factor_of * jnp.repeat(jnp.exp(steps), dims[position] // parts).reshape((-1,) + (1,) * (len(dims) - 1 - position))
    return factor_of


def shared_out(key, own, number, rows, number_of, top, reach, lean):
    ranking = jax.random.permutation(key, number_of)
    crowded, usual = load_shares(number_of, rows * top, reach, lean, True), load_shares(number_of, rows * top, reach, lean, False)
    places = jnp.arange(number_of)

    def named(sizes, turn):
        used = int((sizes > 0).sum())
        fixed = max(1, used // 4)
        moved = fixed + (places - fixed + turn * (used - fixed)) % max(1, number_of - fixed)
        return jnp.zeros((number_of,), jnp.int32).at[ranking[jnp.where(places < fixed, places, moved)]].set(jnp.asarray(sizes, jnp.int32))

    sizes = jnp.where(number % 4 == 0, named(crowded, number // 4), named(usual, number - number // 4 - 1))
    mixed = jax.random.permutation(jax.random.fold_in(own, 3), number_of)
    giver, receiver = mixed[0:number_of // 2 * 2:2], mixed[1:number_of // 2 * 2:2]
    slack = jnp.minimum(sizes[giver] - 1, reach - sizes[receiver]) // 2
    slack = jnp.where((giver == ranking[0]) | (receiver == ranking[0]) | (sizes[receiver] == 0), 0, jnp.maximum(slack, 0))
    moved = jax.random.randint(jax.random.fold_in(own, 4), (number_of // 2,), 0, 1 << 20) % (slack + 1)
    sizes = sizes.at[giver].add(-moved).at[receiver].add(moved)
    labels = jnp.searchsorted(jnp.cumsum(sizes), jnp.arange(rows * top), side="right").astype(jnp.int32)
    listing = labels.reshape(top, rows).T
    listing = listing[jax.random.permutation(jax.random.fold_in(own, 1), rows)]
    turn = jax.random.randint(jax.random.fold_in(own, 2), (rows, 1), 0, top)
    return jnp.take_along_axis(listing, (jnp.arange(top)[None, :] + turn) % top, axis=1)


def load_shares(number_of, total, reach, skew, full):
    weights = [(1 << 20) // math.isqrt(rank ** skew) + 1 for rank in range(1, number_of + 1)]
    largest = reach if full else min(reach, max(-(-total // number_of), total * weights[0] // sum(weights)))
    least = 1 if total - largest >= number_of - 1 else 0
    counts, spare = [largest] + [least] * (number_of - 1), total - largest - least * (number_of - 1)
    while spare > 0:
        movable = [i for i in range(1, number_of) if counts[i] < largest] or [i for i in range(1, number_of) if counts[i] < reach]
        whole, left = sum([weights[i] for i in movable]), spare
        for i in movable:
            addition = min(reach - counts[i], max(1, left * weights[i] // whole), spare)
            counts[i] = counts[i] + addition
            spare = spare - addition
    return np.array(counts)


def centred(own_key, extent, deviation, reach, split=(), kind=jnp.bfloat16):
    loudness = levels(own_key, extent, split, -0.22, 0.18) if split else 1.0
    array = jax.random.normal(own_key, extent, jnp.float32) * deviation * loudness
    return jnp.minimum(jnp.maximum(array, -reach), reach).astype(kind)


def setup_inputs(seed: int = 0) -> dict:
    arg_keys = jax.random.split(jax.random.key(seed), 9)
    frames = centred(arg_keys[0], (FRAMES, D), 1.0, 6.0, ((0, 512),))
    lengths = draw_lengths(jax.random.fold_in(arg_keys[8], 71), 0)
    routes_keys = jax.random.split(jax.random.fold_in(arg_keys[2], 1), FRAMES // TOK_DEV)
    routes_turns = jax.random.permutation(jax.random.fold_in(arg_keys[2], 3), FRAMES // TOK_DEV)
    routes = jax.vmap(lambda own, number: shared_out(jax.random.fold_in(arg_keys[2], 2), own, number, TOK_DEV, EXPERTS, TOP, CAP, 0))(routes_keys, routes_turns).reshape((FRAMES, TOP))
    gate_weights = jnp.clip(0.25 + 0.75 * jax.random.uniform(arg_keys[3], (FRAMES, TOP), jnp.float32) ** levels(arg_keys[3], (FRAMES, TOP), ((0, 512),), -0.2, 0.2), 0.25, 1.0)
    kernel = centred(arg_keys[4], (KW, D), KW ** -0.5, 1.0, (), jnp.float32)
    up_weight = centred(arg_keys[5], (EXPERTS, W, D), D ** -0.5, 0.1875, ((0, 32), (1, 16)))
    down_weight = centred(arg_keys[6], (EXPERTS, W, D), W ** -0.5, 0.125, ((0, 32), (1, 16)))
    cotangent = centred(arg_keys[7], (FRAMES, D), 0.25, 1.5, ((0, 512),))
    return dict(frames=frames, lengths=lengths, routes=routes, gate_weights=gate_weights, kernel=kernel, up_weight=up_weight, down_weight=down_weight, cotangent=cotangent)


norm_eps = 1e-05

def normalize(values):
    center = values - lax.optimization_barrier(jnp.mean(values, axis=-1, keepdims=True))
    inverse = lax.rsqrt(lax.optimization_barrier(jnp.mean(center * center, axis=-1, keepdims=True)) + norm_eps)
    return (center * inverse, inverse)

def norm_back(normed, inverse, upstream):
    mean_grad = lax.optimization_barrier(jnp.mean(upstream, axis=-1, keepdims=True))
    mean_cross = lax.optimization_barrier(jnp.mean(upstream * normed, axis=-1, keepdims=True))
    return inverse * (upstream - mean_grad - normed * mean_cross)

def silu_slope(values):
    sigmoid_part = jax.nn.sigmoid(values)
    return sigmoid_part + values * sigmoid_part * (1.0 - sigmoid_part)

def depthwise(values, kernel):
    kernel_width = kernel.shape[0]
    half_width = kernel_width // 2
    length_rows = values.shape[0]
    padded = jnp.pad(values, ((half_width, half_width), (0, 0)))
    summed = jnp.zeros_like(values)
    for offset in range(kernel_width):
        summed = summed + kernel[offset] * padded[offset:offset + length_rows]
    return summed

def depthwise_back(upstream, kernel):
    kernel_width = kernel.shape[0]
    half_width = kernel_width // 2
    length_rows = upstream.shape[0]
    padded = jnp.pad(upstream, ((half_width, half_width), (0, 0)))
    summed = jnp.zeros_like(upstream)
    for offset in range(kernel_width):
        start_row = 2 * half_width - offset
        summed = summed + kernel[offset] * padded[start_row:start_row + length_rows]
    return summed

def front_pieces(block, length_now, gate_block, kernel):
    positions = jnp.arange(TOK_DEV, dtype=jnp.int32)[:, None]
    live_mask = (positions < length_now).astype(jnp.float32)
    first_hat, first_inv = normalize(block.astype(jnp.float32))
    conv_pre = depthwise(first_hat * live_mask, kernel)
    residual = block.astype(jnp.float32) + jax.nn.silu(conv_pre)
    second_hat, second_inv = normalize(residual)
    live_gate = gate_block * live_mask
    return (live_mask, first_hat, first_inv, conv_pre, residual, second_hat, second_inv, live_gate)

def slot_table(route_block):
    flat_routes = route_block.reshape(-1).astype(jnp.int32)
    one_hot = (flat_routes[:, None] == jnp.arange(EXPERTS, dtype=jnp.int32)[None, :]).astype(jnp.int32)
    rank_of = lax.optimization_barrier(jnp.sum((jnp.cumsum(one_hot, axis=0) - one_hot) * one_hot, axis=1)).astype(jnp.int32)
    return (flat_routes * CAP + rank_of).astype(jnp.int32)

def reference(frames, lengths, routes, gate_weights, kernel, up_weight, down_weight, cotangent):
    device_count = N_EP * N_REP
    pair_count = TOP * TOK_DEV
    frame_blocks = frames.reshape(device_count, TOK_DEV, D)
    route_blocks = routes.reshape(device_count, TOK_DEV, TOP)
    gate_blocks = gate_weights.reshape(device_count, TOK_DEV, TOP)
    cot_blocks = cotangent.reshape(device_count, TOK_DEV, D)

    def front(operands):
        block, length_now, route_block, gate_block, cot_block = operands
        pieces = front_pieces(block, length_now, gate_block, kernel)
        normed = pieces[5].astype(jnp.bfloat16)
        live_gate = pieces[7]
        slot_of = slot_table(route_block)
        source = jnp.zeros((pair_count,), jnp.int32).at[slot_of].set(jnp.arange(pair_count, dtype=jnp.int32))
        cot_pairs = (live_gate[:, :, None] * cot_block.astype(jnp.float32)[:, None, :]).reshape(pair_count, D)
        cot_pairs = cot_pairs.astype(jnp.bfloat16)
        return (normed[source // TOP], cot_pairs[source])
    send_rows, send_slopes = lax.map(front, (frame_blocks, lengths, route_blocks, gate_blocks, cot_blocks))
    rows_in = send_rows.reshape(device_count, EXPERTS, CAP, D).transpose(1, 0, 2, 3).reshape(EXPERTS, device_count * CAP, D)
    slopes_in = send_slopes.reshape(device_count, EXPERTS, CAP, D).transpose(1, 0, 2, 3).reshape(EXPERTS, device_count * CAP, D)

    def expert_pass(operands):
        rows_now, slopes_now, up_rows, down_rows = operands
        pre_hidden = jnp.dot(rows_now, up_rows.T, preferred_element_type=jnp.float32)
        hidden = jax.nn.silu(pre_hidden).astype(jnp.bfloat16)
        expert_out = jnp.dot(hidden, down_rows, preferred_element_type=jnp.float32).astype(jnp.bfloat16)
        hidden_grad = jnp.dot(slopes_now, down_rows.T, preferred_element_type=jnp.float32)
        slopes = (hidden_grad * silu_slope(pre_hidden)).astype(jnp.bfloat16)
        row_grad = jnp.dot(slopes, up_rows, preferred_element_type=jnp.float32).astype(jnp.bfloat16)
        hidden_parts = hidden.reshape(N_EP, N_REP, CAP, W).astype(jnp.float32)
        slope_parts = slopes.reshape(N_EP, N_REP, CAP, W).astype(jnp.float32)
        row_parts = rows_now.reshape(N_EP, N_REP, CAP, D).astype(jnp.float32)
        cot_parts = slopes_now.reshape(N_EP, N_REP, CAP, D).astype(jnp.float32)
        down_parts = jnp.einsum('prcw,prcd->rwd', hidden_parts, cot_parts, precision=lax.Precision.HIGHEST)
        down_parts = lax.optimization_barrier(down_parts.astype(jnp.bfloat16)).astype(jnp.float32)
        up_parts = jnp.einsum('prcw,prcd->rwd', slope_parts, row_parts, precision=lax.Precision.HIGHEST)
        up_parts = lax.optimization_barrier(up_parts.astype(jnp.bfloat16)).astype(jnp.float32)
        return (expert_out, row_grad, lax.optimization_barrier(jnp.sum(up_parts, axis=0)), lax.optimization_barrier(jnp.sum(down_parts, axis=0)))
    expert_out, row_grad, up_grad, down_grad = lax.map(expert_pass, (rows_in, slopes_in, up_weight, down_weight))
    back_out = expert_out.reshape(EXPERTS, device_count, CAP, D).transpose(1, 0, 2, 3).reshape(device_count, EXPERTS * CAP, D)
    back_grad = row_grad.reshape(EXPERTS, device_count, CAP, D).transpose(1, 0, 2, 3).reshape(device_count, EXPERTS * CAP, D)

    def back(operands):
        block, length_now, route_block, gate_block, cot_block, out_slots, grad_slots = operands
        live_mask, first_hat, first_inv, conv_pre, residual, second_hat, second_inv, live_gate = front_pieces(block, length_now, gate_block, kernel)
        slot_of = slot_table(route_block)
        pair_out = out_slots[slot_of].astype(jnp.float32).reshape(TOK_DEV, TOP, D)
        mixture = lax.optimization_barrier(jnp.sum(live_gate[:, :, None] * pair_out, axis=1))
        block_out = (residual + mixture).astype(jnp.bfloat16)
        normed_grad = lax.optimization_barrier(jnp.sum(grad_slots[slot_of].astype(jnp.float32).reshape(TOK_DEV, TOP, D), axis=1))
        residual_grad = cot_block.astype(jnp.float32) + norm_back(second_hat, second_inv, normed_grad)
        conv_grad = residual_grad * silu_slope(conv_pre)
        first_grad = depthwise_back(conv_grad, kernel) * live_mask
        frame_grad = (residual_grad + norm_back(first_hat, first_inv, first_grad)).astype(jnp.bfloat16)
        return (block_out, frame_grad)
    block_out, frame_grad = lax.map(back, (frame_blocks, lengths, route_blocks, gate_blocks, cot_blocks, back_out, back_grad))
    return (block_out.reshape(FRAMES, D), frame_grad.reshape(FRAMES, D), up_grad, down_grad)
```

```python
import functools

import jax
import jax.numpy as jnp
from jax import lax
from jax.experimental import pallas as pl
from jax.experimental.pallas import tpu as pltpu
from jax.sharding import PartitionSpec as P

MESH = pl.DeviceIdType.MESH
DMA = pltpu.SemaphoreType.DMA
F32 = jnp.float32
BF16 = jnp.bfloat16

EPS = 1e-05
SIDE = 4
CAP = 8
TAPS = 31
EDGE = 16
NEAR = ((0, 1), (1, -1))
ORDER = (0, -1, 1, 2)
LEAVE = (2, 1, -1, 0)


def wrap(i, n):
    return lax.rem(i + n, n)


def lane_iota(shape):
    return lax.broadcasted_iota(jnp.int32, shape, 1)


def landed(ref, sem):
    pltpu.make_async_copy(ref, ref, sem).wait()


def route_places(routes_ref, place_ref):
    count = routes_ref.shape[0]
    width = place_ref.shape[2]
    lane = lane_iota((count, 128))
    first, second = routes_ref[:, 0:1], routes_ref[:, 1:2]
    hot = [lane == first, lane == second]
    both = (hot[0].astype(F32) + hot[1].astype(F32)).astype(BF16)
    square = (count, count)
    earlier = lane_iota(square) < lax.broadcasted_iota(jnp.int32, square, 0)
    before = jnp.dot(earlier.astype(F32).astype(BF16), both, preferred_element_type=F32)
    wide = lane_iota((count, width)).astype(F32)
    for k, expert in enumerate((first, second)):
        rank = jnp.sum(jnp.where(hot[k], before, 0.0), axis=1, keepdims=True)
        row = expert.astype(F32) * (2 * CAP) + rank
        place_ref[2 * k] = (wide == row).astype(F32).astype(BF16)
        place_ref[2 * k + 1] = (wide == row + CAP).astype(F32).astype(BF16)


def contract_first(left, right):
    return lax.dot_general(left, right, (((0,), (0,)), ((), ())), preferred_element_type=F32)


def contract_last(left, right):
    return lax.dot_general(left, right, (((1,), (1,)), ((), ())), preferred_element_type=F32)


def pack_slopes(cot_ref, gate_ref, place_ref, out_ref):
    count, width = cot_ref.shape
    half = width // 2
    cot = cot_ref[...].astype(F32)
    parts = []
    for k in range(2):
        scaled = (gate_ref[:, k : k + 1] * cot).astype(BF16)
        parts += [scaled[:, :half], scaled[:, half:]]
    stacked = jnp.concatenate(parts, axis=0)
    place = place_ref[...].reshape(4 * count, -1)
    out_ref[...] = contract_first(place, stacked).astype(BF16).reshape(out_ref.shape)


def pack_rows(normed_ref, place_ref, out_ref):
    count, width = normed_ref.shape
    half = width // 2
    stacked = jnp.concatenate([normed_ref[:, :half], normed_ref[:, half:]], axis=0)
    low = place_ref[0] + place_ref[2]
    high = place_ref[1] + place_ref[3]
    place = jnp.concatenate([low, high], axis=0)
    out_ref[...] = contract_first(place, stacked).astype(BF16).reshape(out_ref.shape)


def over_rows(count, step, body):
    def run(i, carry):
        body(pl.ds(pl.multiple_of(i * step, step), step), pl.multiple_of(i * step, step))
        return carry

    lax.fori_loop(0, count // step, run, 0)


def normalize(values):
    center = values - jnp.mean(values, axis=-1, keepdims=True)
    inverse = lax.rsqrt(jnp.mean(center * center, axis=-1, keepdims=True) + EPS)
    return center * inverse, inverse


def norm_back(normed, inverse, upstream):
    mean_grad = jnp.mean(upstream, axis=-1, keepdims=True)
    mean_cross = jnp.mean(upstream * normed, axis=-1, keepdims=True)
    return inverse * (upstream - mean_grad - normed * mean_cross)


def silu_slope(values):
    part = jax.nn.sigmoid(values)
    return part + values * part * (1.0 - part)


def depthwise(pad_ref, kernel_ref, out_ref, reverse):
    count, width = out_ref.shape
    columns = 128

    def run(i, carry):
        at = pl.ds(pl.multiple_of(i * columns, columns), columns)
        total = jnp.zeros((count, columns), F32)
        for shift in range(8):
            part = None
            for base in range(0, 32, 8):
                j = base + shift - 1
                if j < 0 or j >= TAPS:
                    continue
                row = TAPS - 1 - j if reverse else j
                term = kernel_ref[row : row + 1, at] * pad_ref[base : base + count + 8, at]
                part = term if part is None else part + term
            if shift:
                part = pltpu.roll(part, count + 8 - shift, 0)
            total = total + part[:count]
        out_ref[:, at] = total
        return carry

    lax.fori_loop(0, width // columns, run, 0)


def front_norm(frames_ref, mask_ref, hat_ref, inv_ref, pad_ref):
    count, width = frames_ref.shape
    pad_ref[:EDGE] = jnp.zeros((EDGE, width), F32)
    pad_ref[EDGE + count :] = jnp.zeros((EDGE, width), F32)

    def body(at, start):
        hat, inverse = normalize(frames_ref[at].astype(F32))
        hat_ref[at] = hat
        inv_ref[at] = inverse
        pad_ref[pl.ds(start + EDGE, 16)] = hat * mask_ref[at]

    over_rows(count, 16, body)


def front_residual(frames_ref, conv_ref, res_ref, hat_ref, inv_ref, normed_ref):
    def body(at, start):
        residual = frames_ref[at].astype(F32) + jax.nn.silu(conv_ref[at])
        hat, inverse = normalize(residual)
        res_ref[at] = residual
        hat_ref[at] = hat
        inv_ref[at] = inverse
        normed_ref[at] = hat.astype(BF16)

    over_rows(frames_ref.shape[0], 16, body)


def back_mix(back_ref, place_ref, gate_ref, res_ref, out_ref):
    half = back_ref.shape[2]
    rows = back_ref[...].reshape(-1, half)
    for h in range(2):
        at = slice(h * half, (h + 1) * half)
        mixed = gate_ref[:, 0:1] * jnp.dot(place_ref[h], rows, preferred_element_type=F32)
        mixed += gate_ref[:, 1:2] * jnp.dot(place_ref[2 + h], rows, preferred_element_type=F32)
        out_ref[:, at] = (res_ref[:, at] + mixed).astype(BF16)


def back_slopes(back_ref, place_ref, grad_ref):
    half = back_ref.shape[2]
    rows = back_ref[...].reshape(-1, half)
    for h in range(2):
        pick = place_ref[h] + place_ref[2 + h]
        grad_ref[:, h * half : (h + 1) * half] = jnp.dot(pick, rows, preferred_element_type=F32)


def back_residual(cot_ref, hat_ref, inv_ref, conv_ref, grad_ref, pad_ref):
    def body(at, start):
        grad = cot_ref[at].astype(F32) + norm_back(hat_ref[at], inv_ref[at], grad_ref[at])
        grad_ref[at] = grad
        pad_ref[pl.ds(start + EDGE, 16)] = grad * silu_slope(conv_ref[at])

    over_rows(cot_ref.shape[0], 16, body)


def back_frames(first_ref, mask_ref, hat_ref, inv_ref, grad_ref, out_ref):
    def body(at, start):
        first = first_ref[at] * mask_ref[at]
        out_ref[at] = (grad_ref[at] + norm_back(hat_ref[at], inv_ref[at], first)).astype(BF16)

    over_rows(out_ref.shape[0], 16, body)


class Ring:
    def __init__(self, x_first):
        rep = lax.axis_index("rep")
        x, y = lax.rem(rep, SIDE), lax.div(rep, SIDE)
        self.x_first = x_first
        self.ep = lax.axis_index("ep")
        self.first, self.second = (x, y) if x_first else (y, x)
        self.started = []

    def index(self, first, second):
        first, second = wrap(first, SIDE), wrap(second, SIDE)
        return second * SIDE + first if self.x_first else first * SIDE + second

    def here(self):
        return self.index(self.first, self.second)

    def send(self, src, dst, send_sem, recv_sem, target):
        copy = pltpu.make_async_remote_copy(
            src_ref=src,
            dst_ref=dst,
            send_sem=send_sem,
            recv_sem=recv_sem,
            device_id=(self.ep, target),
            device_id_type=MESH,
        )
        copy.start()
        self.started.append(copy)

    def finish(self):
        for copy in self.started:
            copy.wait_send()


class Gather(Ring):
    def __init__(self, x_first, full, send_sem, near_sem, far_sem, row_sem, row_far_sem):
        super().__init__(x_first)
        self.full, self.send_sem = full, send_sem
        self.near_sem, self.far_sem = near_sem, far_sem
        self.row_sem, self.row_far_sem = row_sem, row_far_sem
        self.half = full.shape[1] // 2

    def piece(self, block, half):
        if half is None:
            return self.full.at[block]
        return self.full.at[block, pl.ds(half * self.half, self.half)]

    def push(self, block, half, target, sem):
        ref = self.piece(block, half)
        self.send(ref, ref, self.send_sem.at[len(self.started)], sem, target)

    def start(self):
        block = self.here()
        for d, s in NEAR:
            self.push(block, None, self.index(self.first + s, self.second), self.near_sem.at[d])
        self.across(0)

    def across(self, k):
        block = self.index(self.first + ORDER[k], self.second)
        for d, s in NEAR:
            self.push(block, None, self.index(self.first, self.second + s), self.row_sem.at[d, k])

    def relay_near(self):
        for d, s in NEAR:
            block = self.index(self.first - s, self.second)
            landed(self.piece(block, None), self.near_sem.at[d])
            self.push(block, d, self.index(self.first + s, self.second), self.far_sem.at[d])
            self.across(1 + d)

    def relay_far(self):
        block = self.index(self.first + 2, self.second)
        for d in (0, 1):
            landed(self.piece(block, d), self.far_sem.at[d])
        self.across(3)

    def relay_row(self, k):
        for d, s in NEAR:
            block = self.index(self.first + ORDER[k], self.second - s)
            landed(self.piece(block, None), self.row_sem.at[d, k])
            target = self.index(self.first, self.second + s)
            self.push(block, d, target, self.row_far_sem.at[d, k])

    def end_row(self, k):
        block = self.index(self.first + ORDER[k], self.second + 2)
        for d in (0, 1):
            landed(self.piece(block, d), self.row_far_sem.at[d, k])


class Scatter(Ring):
    def __init__(self, x_first, parts, via, near, part, via_last, near_last, *sems):
        super().__init__(x_first)
        self.parts, self.via, self.near, self.part = parts, via, near, part
        self.via_last, self.near_last = via_last, near_last
        self.sems = sems
        self.half = parts.shape[1] // 2

    def rows(self, half):
        return pl.ds(half * self.half, self.half)

    def block(self, step, i):
        return self.index(self.first + step, self.second + LEAVE[i])

    def send_far(self, i):
        send_sem, recv_sem = self.sems[0], self.sems[1]
        block = self.block(2, i)
        for d, s in NEAR:
            self.send(
                self.parts.at[block, self.rows(1 - d)],
                self.via.at[d, i],
                send_sem.at[d, i],
                recv_sem.at[d, i],
                self.index(self.first + s, self.second),
            )

    def send_near(self, d, i):
        send_sem, recv_sem = self.sems[2], self.sems[3]
        s = NEAR[d][1]
        block = self.block(s, i)
        landed(self.via.at[d, i], self.sems[1].at[d, i])
        rows = self.rows(1 - d)
        mine = self.parts[block, rows].astype(F32)
        self.parts[block, rows] = (mine + self.via[d, i].astype(F32)).astype(BF16)
        self.send(
            self.parts.at[block],
            self.near.at[d, i],
            send_sem.at[d, i],
            recv_sem.at[d, i],
            self.index(self.first + s, self.second),
        )

    def total(self, i):
        for d in (0, 1):
            landed(self.near.at[d, i], self.sems[3].at[d, i])
        mine = self.parts[self.block(0, i)].astype(F32)
        return mine + self.near[0, i].astype(F32) + self.near[1, i].astype(F32)

    def keep(self, i):
        self.part[i] = self.total(i).astype(BF16)

    def send_far_last(self):
        send_sem, recv_sem = self.sems[4], self.sems[5]
        for d, s in NEAR:
            self.send(
                self.part.at[0, self.rows(1 - d)],
                self.via_last.at[d],
                send_sem.at[d],
                recv_sem.at[d],
                self.index(self.first, self.second + s),
            )

    def send_near_last(self):
        send_sem, recv_sem = self.sems[6], self.sems[7]
        for d, s in NEAR:
            landed(self.via_last.at[d], self.sems[5].at[d])
            rows = self.rows(1 - d)
            mine = self.part[1 + d, rows].astype(F32)
            self.part[1 + d, rows] = (mine + self.via_last[d].astype(F32)).astype(BF16)
            self.send(
                self.part.at[1 + d],
                self.near_last.at[d],
                send_sem.at[d],
                recv_sem.at[d],
                self.index(self.first, self.second + s),
            )

    def last(self, out_ref):
        for d in (0, 1):
            landed(self.near_last.at[d], self.sems[7].at[d])
        mine = self.total(3)
        out_ref[...] = mine + self.near_last[0].astype(F32) + self.near_last[1].astype(F32)


class Exchange:
    def __init__(self, count, send, recv, send_sem, recv_sem):
        self.count = count
        self.send, self.recv = send, recv
        self.send_sem, self.recv_sem = send_sem, recv_sem
        self.ep, self.rep = lax.axis_index("ep"), lax.axis_index("rep")

    def copy(self, other, place):
        return pltpu.make_async_remote_copy(
            src_ref=self.send.at[other],
            dst_ref=self.recv.at[place],
            send_sem=self.send_sem.at[other],
            recv_sem=self.recv_sem.at[place],
            device_id=(other, self.rep),
            device_id_type=MESH,
        )

    def each(self, body):
        def run(i, carry):
            body(lax.rem(self.ep + i, self.count))
            return carry

        lax.fori_loop(1, self.count, run, 0)

    def start(self):
        self.each(lambda other: self.copy(other, self.ep).start())
        self.recv[self.ep] = self.send[self.ep]

    def arrive(self):
        self.each(lambda other: self.copy(other, other).wait_recv())

    def finish(self):
        self.each(lambda other: self.copy(other, other).wait_send())


def enter(count):
    ep, rep = lax.axis_index("ep"), lax.axis_index("rep")
    barrier = pltpu.get_barrier_semaphore()

    def run(i, carry):
        other = lax.rem(ep + i, count)
        pl.semaphore_signal(barrier, inc=1, device_id=(other, rep), device_id_type=MESH)
        return carry

    lax.fori_loop(1, count, run, 0)
    ring = Ring(True)
    for _, s in NEAR:
        for target in (ring.index(ring.first + s, ring.second), ring.index(ring.first, ring.second + s)):
            pl.semaphore_signal(barrier, inc=1, device_id=(ep, target), device_id_type=MESH)
    pl.semaphore_wait(barrier, count - 1 + 4)


def unpack(packed_ref, rows_ref):
    count, _, half = packed_ref.shape
    step = 4

    def run(i, carry):
        block = packed_ref[pl.ds(i * step, step)].astype(F32)
        at = pl.ds(pl.multiple_of(i * step * CAP, step * CAP), step * CAP)
        rows_ref[at, :half] = block[:, :CAP].reshape(step * CAP, half).astype(BF16)
        rows_ref[at, half:] = block[:, CAP:].reshape(step * CAP, half).astype(BF16)
        return carry

    lax.fori_loop(0, count // step, run, 0)


def pack(rows_ref, packed_ref):
    count, _, half = packed_ref.shape
    step = 4

    def run(i, carry):
        block = rows_ref[pl.ds(pl.multiple_of(i * step * CAP, step * CAP), step * CAP)]
        block = block.reshape(step, CAP, 2 * half)
        both = jnp.concatenate([block[:, :, :half], block[:, :, half:]], axis=1)
        packed_ref[pl.ds(i * step, step)] = both.astype(BF16)
        return carry

    lax.fori_loop(0, count // step, run, 0)


def weight_rows(weight_ref, j):
    pair = weight_ref[pl.ds(2 * j, 2)]
    return pair.reshape(2 * pair.shape[1], pair.shape[2])


def hidden_grads(slopes_in_ref, down_ref, wide_ref):
    def run(j, carry):
        wide_ref[j] = contract_last(slopes_in_ref[...], weight_rows(down_ref, j))
        return carry

    lax.fori_loop(0, wide_ref.shape[0], run, 0)


def hidden_units(rows_ref, up_ref, down_ref, wide_ref, hidden_ref, slopes_ref, out_ref, grad_ref):
    unit = hidden_ref.shape[2]
    out_ref[...] = jnp.zeros_like(out_ref)
    grad_ref[...] = jnp.zeros_like(grad_ref)

    def run(j, carry):
        pre = contract_last(rows_ref[...], weight_rows(up_ref, j))
        part = jax.nn.sigmoid(pre)
        hidden = (pre * part).astype(BF16)
        slopes = (wide_ref[j] * (part + pre * part * (1.0 - part))).astype(BF16)
        for i in range(2):
            hidden_ref[2 * j + i] = hidden[:, i * unit : (i + 1) * unit]
            slopes_ref[2 * j + i] = slopes[:, i * unit : (i + 1) * unit]
        out_ref[...] += jnp.dot(hidden, weight_rows(down_ref, j), preferred_element_type=F32)
        grad_ref[...] += jnp.dot(slopes, weight_rows(up_ref, j), preferred_element_type=F32)
        return carry

    lax.fori_loop(0, wide_ref.shape[0], run, 0)


def weight_grads(scatter, step, left_ref, right_ref):
    def run(i, carry):
        block = scatter.index(scatter.first + step, i)
        grads = contract_first(left_ref[block], right_ref[...])
        scatter.parts[block] = grads.astype(BF16)
        return carry

    lax.fori_loop(0, SIDE, run, 0)


def block_kernel(count, *refs):
    names = iter(refs)

    def take(n):
        return [next(names) for _ in range(n)]

    frames, mask, routes, gates, kernel, up_shard, down_shard, cot = take(8)
    block_out, frame_grad, up_grad, down_grad = take(4)
    up_all, down_all, local_sem = take(3)
    place, normed, hat1, inv1, pad, conv, res, hat2, inv2 = take(9)
    send_slopes, send_rows, recv_slopes, recv_rows = take(4)
    back_out, back_grad, recv_out, recv_grad = take(4)
    slopes_in, rows_in, wide, hidden, slopes, out_sum, grad_sum = take(7)
    normed_grad, first_grad = take(2)
    up_parts, down_parts = take(2)
    up_room, down_room = take(5), take(5)
    exchange_sems = [take(2) for _ in range(4)]
    gather_sems = [take(5) for _ in range(2)]
    scatter_sems = [take(8) for _ in range(2)]

    rep = lax.axis_index("rep")
    own = [
        pltpu.make_async_copy(up_shard, up_all.at[rep], local_sem.at[0]),
        pltpu.make_async_copy(down_shard, down_all.at[rep], local_sem.at[1]),
    ]
    for copy in own:
        copy.start()
    enter(count)
    for copy in own:
        copy.wait()
    gathers = [Gather(True, up_all, *gather_sems[0]), Gather(False, down_all, *gather_sems[1])]
    for gather in gathers:
        gather.start()

    to_slopes = Exchange(count, send_slopes, recv_slopes, *exchange_sems[0])
    to_rows = Exchange(count, send_rows, recv_rows, *exchange_sems[1])
    to_out = Exchange(count, back_out, recv_out, *exchange_sems[2])
    to_grad = Exchange(count, back_grad, recv_grad, *exchange_sems[3])

    route_places(routes, place)
    pack_slopes(cot, gates, place, send_slopes)
    to_slopes.start()
    front_norm(frames, mask, hat1, inv1, pad)
    depthwise(pad, kernel, conv, False)
    front_residual(frames, conv, res, hat2, inv2, normed)
    pack_rows(normed, place, send_rows)
    to_rows.start()

    for gather in gathers:
        gather.relay_near()
    for gather in gathers:
        gather.relay_row(0)
    for gather in gathers:
        gather.relay_far()
    for k in (1, 2, 3):
        for gather in gathers:
            gather.relay_row(k)
    to_slopes.arrive()
    unpack(recv_slopes, slopes_in)
    for k in range(SIDE):
        for gather in gathers:
            gather.end_row(k)
    hidden_grads(slopes_in, down_all, wide)
    to_rows.arrive()
    unpack(recv_rows, rows_in)
    hidden_units(rows_in, up_all, down_all, wide, hidden, slopes, out_sum, grad_sum)
    pack(out_sum, back_out)
    to_out.start()
    pack(grad_sum, back_grad)
    to_grad.start()

    scatters = [
        Scatter(False, up_parts, *up_room, *scatter_sems[0]),
        Scatter(True, down_parts, *down_room, *scatter_sems[1]),
    ]
    sides = [(slopes, rows_in), (hidden, slopes_in)]
    for scatter, (left, right) in zip(scatters, sides):
        weight_grads(scatter, 2, left, right)
        for i in range(SIDE):
            scatter.send_far(i)
    for step in (1, -1, 0):
        for scatter, (left, right) in zip(scatters, sides):
            weight_grads(scatter, step, left, right)
    for i in range(SIDE):
        for scatter in scatters:
            for d in (0, 1):
                scatter.send_near(d, i)
    for i in range(3):
        for scatter in scatters:
            scatter.keep(i)
            if i == 0:
                scatter.send_far_last()
    for scatter in scatters:
        scatter.send_near_last()

    to_out.arrive()
    back_mix(recv_out, place, gates, res, block_out)
    to_grad.arrive()
    back_slopes(recv_grad, place, normed_grad)
    back_residual(cot, hat2, inv2, conv, normed_grad, pad)
    depthwise(pad, kernel, first_grad, True)
    back_frames(first_grad, mask, hat1, inv1, normed_grad, frame_grad)
    for scatter, out in zip(scatters, (up_grad, down_grad)):
        scatter.last(out)

    for exchange in (to_slopes, to_rows, to_out, to_grad):
        exchange.finish()
    for ring in gathers + scatters:
        ring.finish()


def on_device(frames, lengths, routes, gate_weights, kernel, up_weight, down_weight, cotangent):
    experts = lax.axis_size("ep")
    reps = lax.axis_size("rep")
    count, width = frames.shape
    unit = up_weight.shape[1]
    rows = experts * CAP
    half = width // 2
    positions = lax.broadcasted_iota(jnp.int32, (count, 1), 0)
    mask = (positions < lengths[0]).astype(F32)
    gates = gate_weights * mask

    vmem = pltpu.VMEM
    packed = vmem((experts, 2 * CAP, half), BF16)
    grid32 = vmem((count, width), F32)
    column = vmem((count, 1), F32)
    weights = vmem((reps, unit, width), BF16)
    room = [
        vmem((2, SIDE, unit // 2, width), BF16),
        vmem((2, SIDE, unit, width), BF16),
        vmem((3, unit, width), BF16),
        vmem((2, unit // 2, width), BF16),
        vmem((2, unit, width), BF16),
    ]
    scratch = [weights, weights, DMA((2,))]
    scratch += [vmem((4, count, 2 * rows), BF16), vmem((count, width), BF16)]
    scratch += [grid32, column, vmem((count + 2 * EDGE, width), F32), grid32, grid32, grid32, column]
    scratch += [packed] * 8
    scratch += [vmem((rows, width), BF16)] * 2
    scratch += [vmem((reps // 2, rows, 2 * unit), F32)]
    scratch += [vmem((reps, rows, unit), BF16)] * 2
    scratch += [vmem((rows, width), F32)] * 2
    scratch += [grid32, grid32, weights, weights] + room + room
    scratch += [DMA((experts,))] * 8
    scratch += [DMA((20,)), DMA((2,)), DMA((2,)), DMA((2, SIDE)), DMA((2, SIDE))] * 2
    scratch += ([DMA((2, SIDE))] * 4 + [DMA((2,))] * 4) * 2

    in_vmem = pl.BlockSpec(memory_space=pltpu.VMEM)
    anywhere = pl.BlockSpec(memory_space=pl.ANY)
    block_out, frame_grad, up_grad, down_grad = pl.pallas_call(
        functools.partial(block_kernel, experts),
        out_shape=[jax.ShapeDtypeStruct((count, width), BF16)] * 2
        + [jax.ShapeDtypeStruct((unit, width), F32)] * 2,
        in_specs=[in_vmem] * 5 + [anywhere] * 2 + [in_vmem],
        out_specs=[in_vmem] * 4,
        scratch_shapes=scratch,
        compiler_params=pltpu.CompilerParams(
            collective_id=0, has_side_effects=True, vmem_limit_bytes=58 << 20
        ),
        cost_estimate=pl.CostEstimate(
            flops=12 * rows * reps * unit * width, bytes_accessed=8 << 20, transcendentals=0
        ),
    )(frames, mask, routes, gates, kernel, up_weight[0], down_weight[0], cotangent)
    return block_out, frame_grad, up_grad[None], down_grad[None]


def solution(mesh):
    in_specs = (
        P(("ep", "rep"), None),
        P(("ep", "rep")),
        P(("ep", "rep"), None),
        P(("ep", "rep"), None),
        P(),
        P("ep", "rep", None),
        P("ep", "rep", None),
        P(("ep", "rep"), None),
    )
    out_specs = (
        P(("ep", "rep"), None),
        P(("ep", "rep"), None),
        P("ep", "rep", None),
        P("ep", "rep", None),
    )
    return jax.shard_map(
        on_device, mesh=mesh, in_specs=in_specs, out_specs=out_specs, check_vma=False
    )
```

```python
import functools

import jax
import jax.numpy as jnp
from jax import lax
from jax.experimental import pallas as pl
from jax.experimental.pallas import tpu as pltpu
from jax.sharding import PartitionSpec as P

MESH = pl.DeviceIdType.MESH
DMA = pltpu.SemaphoreType.DMA
F32 = jnp.float32
BF16 = jnp.bfloat16

EPS = 1e-05
SIDE = 4
CAP = 8
TAPS = 31
EDGE = 16
NEAR = ((0, 1), (1, -1))
ORDER = (0, -1, 1, 2)
LEAVE = (2, 1, -1, 0)


def wrap(i, n):
    return lax.rem(i + n, n)


def lane_iota(shape):
    return lax.broadcasted_iota(jnp.int32, shape, 1)


def landed(ref, sem):
    pltpu.make_async_copy(ref, ref, sem).wait()


def to_column(row):
    count = row.shape[1]
    square = (count, count)
    here = lane_iota(square) == lax.broadcasted_iota(jnp.int32, square, 0)
    return jnp.sum(jnp.where(here, row, 0.0), axis=1, keepdims=True)


def route_places(routes_ref, rank_ref, place_ref):
    experts = place_ref.shape[0] // (2 * CAP)
    count = routes_ref.shape[1]
    shape = (experts, count)
    sub = lax.broadcasted_iota(jnp.int32, shape, 0)
    hot = [sub == routes_ref[k : k + 1] for k in range(2)]
    both = (hot[0].astype(F32) + hot[1].astype(F32)).astype(BF16)
    square = (count, count)
    earlier = lax.broadcasted_iota(jnp.int32, square, 0) < lane_iota(square)
    before = jnp.dot(both, earlier.astype(F32).astype(BF16), preferred_element_type=F32)
    tall = lax.broadcasted_iota(jnp.int32, (place_ref.shape[0], count), 0).astype(F32)
    for k in range(2):
        rank = jnp.sum(jnp.where(hot[k], before, 0.0), axis=0, keepdims=True)
        row = routes_ref[k : k + 1].astype(F32) * (2 * CAP) + rank
        rank_ref[k : k + 1] = row
        for h in range(2):
            at = slice((2 * k + h) * count, (2 * k + h + 1) * count)
            place_ref[:, at] = (tall == row + h * CAP).astype(F32).astype(BF16)


def turn_places(rank_ref, turned_ref):
    _, count, width = turned_ref.shape
    wide = lane_iota((count, width)).astype(F32)
    for k in range(2):
        row = to_column(rank_ref[k : k + 1])
        for h in range(2):
            turned_ref[2 * k + h] = (wide == row + h * CAP).astype(F32).astype(BF16)


def live_columns(length_ref, gates_ref, mask_ref, gate_ref):
    count = mask_ref.shape[0]
    positions = lax.broadcasted_iota(jnp.int32, (count, 1), 0)
    mask = (positions < length_ref[...]).astype(F32)
    mask_ref[...] = mask
    for k in range(2):
        gate_ref[k] = to_column(gates_ref[k : k + 1]) * mask


def contract_first(left, right):
    return lax.dot_general(left, right, (((0,), (0,)), ((), ())), preferred_element_type=F32)


def contract_last(left, right):
    return lax.dot_general(left, right, (((1,), (1,)), ((), ())), preferred_element_type=F32)


def pack_slopes(cot_ref, gate_ref, place_ref, out_ref):
    width = cot_ref.shape[1]
    half = width // 2
    cot = cot_ref[...].astype(F32)
    parts = []
    for k in range(2):
        scaled = (gate_ref[k] * cot).astype(BF16)
        parts += [scaled[:, :half], scaled[:, half:]]
    stacked = jnp.concatenate(parts, axis=0)
    packed = jnp.dot(place_ref[...], stacked, preferred_element_type=F32)
    out_ref[...] = packed.astype(BF16).reshape(out_ref.shape)


def pack_rows(normed_ref, place_ref, out_ref):
    width = normed_ref.shape[1]
    half = width // 2
    stacked = jnp.concatenate([normed_ref[:, :half], normed_ref[:, half:]], axis=0)
    middle = place_ref.shape[1] // 2
    place = place_ref[:, :middle] + place_ref[:, middle:]
    packed = jnp.dot(place, stacked, preferred_element_type=F32)
    out_ref[...] = packed.astype(BF16).reshape(out_ref.shape)


def over_rows(count, step, body):
    def run(i, carry):
        body(pl.ds(pl.multiple_of(i * step, step), step), pl.multiple_of(i * step, step))
        return carry

    lax.fori_loop(0, count // step, run, 0)


def normalize(values):
    center = values - jnp.mean(values, axis=-1, keepdims=True)
    inverse = lax.rsqrt(jnp.mean(center * center, axis=-1, keepdims=True) + EPS)
    return center * inverse, inverse


def norm_back(normed, inverse, upstream):
    mean_grad = jnp.mean(upstream, axis=-1, keepdims=True)
    mean_cross = jnp.mean(upstream * normed, axis=-1, keepdims=True)
    return inverse * (upstream - mean_grad - normed * mean_cross)


def silu_slope(values):
    part = jax.nn.sigmoid(values)
    return part + values * part * (1.0 - part)


def depthwise(pad_ref, kernel_ref, out_ref, reverse):
    count, width = out_ref.shape
    columns = 128

    def run(i, carry):
        at = pl.ds(pl.multiple_of(i * columns, columns), columns)
        total = jnp.zeros((count, columns), F32)
        for shift in range(8):
            part = None
            for base in range(0, 32, 8):
                j = base + shift - 1
                if j < 0 or j >= TAPS:
                    continue
                row = TAPS - 1 - j if reverse else j
                term = kernel_ref[row : row + 1, at] * pad_ref[base : base + count + 8, at]
                part = term if part is None else part + term
            if shift:
                part = pltpu.roll(part, count + 8 - shift, 0)
            total = total + part[:count]
        out_ref[:, at] = total
        return carry

    lax.fori_loop(0, width // columns, run, 0)


def front_norm(frames_ref, mask_ref, hat_ref, inv_ref, pad_ref):
    count, width = frames_ref.shape
    pad_ref[:EDGE] = jnp.zeros((EDGE, width), F32)
    pad_ref[EDGE + count :] = jnp.zeros((EDGE, width), F32)

    def body(at, start):
        hat, inverse = normalize(frames_ref[at].astype(F32))
        hat_ref[at] = hat
        inv_ref[at] = inverse
        pad_ref[pl.ds(start + EDGE, 16)] = hat * mask_ref[at]

    over_rows(count, 16, body)


def front_residual(frames_ref, conv_ref, res_ref, hat_ref, inv_ref, normed_ref):
    def body(at, start):
        residual = frames_ref[at].astype(F32) + jax.nn.silu(conv_ref[at])
        hat, inverse = normalize(residual)
        res_ref[at] = residual
        hat_ref[at] = hat
        inv_ref[at] = inverse
        normed_ref[at] = hat.astype(BF16)

    over_rows(frames_ref.shape[0], 16, body)


def back_mix(back_ref, place_ref, gate_ref, res_ref, out_ref):
    half = back_ref.shape[2]
    rows = back_ref[...].reshape(-1, half)
    for h in range(2):
        at = slice(h * half, (h + 1) * half)
        mixed = gate_ref[0] * jnp.dot(place_ref[h], rows, preferred_element_type=F32)
        mixed += gate_ref[1] * jnp.dot(place_ref[2 + h], rows, preferred_element_type=F32)
        out_ref[:, at] = (res_ref[:, at] + mixed).astype(BF16)


def back_slopes(back_ref, place_ref, grad_ref):
    half = back_ref.shape[2]
    rows = back_ref[...].reshape(-1, half)
    for h in range(2):
        pick = place_ref[h] + place_ref[2 + h]
        grad_ref[:, h * half : (h + 1) * half] = jnp.dot(pick, rows, preferred_element_type=F32)


def back_residual(cot_ref, hat_ref, inv_ref, conv_ref, grad_ref, pad_ref):
    def body(at, start):
        grad = cot_ref[at].astype(F32) + norm_back(hat_ref[at], inv_ref[at], grad_ref[at])
        grad_ref[at] = grad
        pad_ref[pl.ds(start + EDGE, 16)] = grad * silu_slope(conv_ref[at])

    over_rows(cot_ref.shape[0], 16, body)


def back_frames(first_ref, mask_ref, hat_ref, inv_ref, grad_ref, out_ref):
    def body(at, start):
        first = first_ref[at] * mask_ref[at]
        out_ref[at] = (grad_ref[at] + norm_back(hat_ref[at], inv_ref[at], first)).astype(BF16)

    over_rows(out_ref.shape[0], 16, body)


class Ring:
    def __init__(self, x_first):
        rep = lax.axis_index("rep")
        x, y = lax.rem(rep, SIDE), lax.div(rep, SIDE)
        self.x_first = x_first
        self.ep = lax.axis_index("ep")
        self.first, self.second = (x, y) if x_first else (y, x)

    def device(self, first, second):
        first, second = wrap(first, SIDE), wrap(second, SIDE)
        return second * SIDE + first if self.x_first else first * SIDE + second

    def here(self):
        return self.slot(self.first, self.second)

    def slot(self, first, second):
        return wrap(first, SIDE) * SIDE + wrap(second, SIDE)

    def send(self, src, dst, recv_sem, target):
        pltpu.make_async_remote_copy(
            src_ref=src,
            dst_ref=dst,
            send_sem=self.send_sem.at[0],
            recv_sem=recv_sem,
            device_id=(self.ep, target),
            device_id_type=MESH,
        ).start()

    def finish(self, blocks):
        landed(blocks.at[pl.ds(0, SIDE * SIDE - 1)], self.send_sem.at[0])


class Gather(Ring):
    def __init__(self, x_first, full, send_sem, near_sem, far_sem, row_sem, row_far_sem):
        super().__init__(x_first)
        self.full, self.send_sem = full, send_sem
        self.near_sem, self.far_sem = near_sem, far_sem
        self.row_sem, self.row_far_sem = row_sem, row_far_sem
        self.half = full.shape[1] // 2

    def piece(self, block, half):
        if half is None:
            return self.full.at[block]
        return self.full.at[block, pl.ds(half * self.half, self.half)]

    def push(self, block, half, target, sem):
        ref = self.piece(block, half)
        self.send(ref, ref, sem, target)

    def start(self):
        block = self.here()
        for d, s in NEAR:
            self.push(block, None, self.device(self.first + s, self.second), self.near_sem.at[d])
        self.across(0)

    def across(self, k):
        block = self.slot(self.first + ORDER[k], self.second)
        for d, s in NEAR:
            target = self.device(self.first, self.second + s)
            self.push(block, None, target, self.row_sem.at[d, k])

    def relay_near(self):
        for d, s in NEAR:
            block = self.slot(self.first - s, self.second)
            landed(self.piece(block, None), self.near_sem.at[d])
            self.push(block, d, self.device(self.first + s, self.second), self.far_sem.at[d])
            self.across(1 + d)

    def relay_far(self):
        block = self.slot(self.first + 2, self.second)
        for d in (0, 1):
            landed(self.piece(block, d), self.far_sem.at[d])
        self.across(3)

    def relay_row(self, k):
        for d, s in NEAR:
            block = self.slot(self.first + ORDER[k], self.second - s)
            landed(self.piece(block, None), self.row_sem.at[d, k])
            target = self.device(self.first, self.second + s)
            self.push(block, d, target, self.row_far_sem.at[d, k])

    def end_row(self, k):
        block = self.slot(self.first + ORDER[k], self.second + 2)
        for d in (0, 1):
            landed(self.piece(block, d), self.row_far_sem.at[d, k])


class Scatter(Ring):
    def __init__(self, x_first, parts, via, near, part, via_last, near_last, send_sem, *sems):
        super().__init__(x_first)
        self.parts, self.via, self.near, self.part = parts, via, near, part
        self.via_last, self.near_last = via_last, near_last
        self.send_sem = send_sem
        self.via_sem, self.near_sem, self.via_last_sem, self.near_last_sem = sems
        self.half = parts.shape[1] // 2

    def rows(self, half):
        return pl.ds(half * self.half, self.half)

    def block(self, step, i):
        return self.slot(self.first + step, self.second + LEAVE[i])

    def send_far(self, i):
        block = self.block(2, i)
        for d, s in NEAR:
            target = self.device(self.first + s, self.second)
            src = self.parts.at[block, self.rows(1 - d)]
            self.send(src, self.via.at[d, i], self.via_sem.at[d, i], target)

    def send_near(self, d, i):
        s = NEAR[d][1]
        block = self.block(s, i)
        landed(self.via.at[d, i], self.via_sem.at[d, i])
        rows = self.rows(1 - d)
        mine = self.parts[block, rows].astype(F32)
        self.parts[block, rows] = (mine + self.via[d, i].astype(F32)).astype(BF16)
        target = self.device(self.first + s, self.second)
        self.send(self.parts.at[block], self.near.at[d, i], self.near_sem.at[d, i], target)

    def total(self, i):
        for d in (0, 1):
            landed(self.near.at[d, i], self.near_sem.at[d, i])
        mine = self.parts[self.block(0, i)].astype(F32)
        return mine + self.near[0, i].astype(F32) + self.near[1, i].astype(F32)

    def keep(self, i):
        self.part[i] = self.total(i).astype(BF16)

    def send_far_last(self):
        for d, s in NEAR:
            target = self.device(self.first, self.second + s)
            src = self.part.at[0, self.rows(1 - d)]
            self.send(src, self.via_last.at[d], self.via_last_sem.at[d], target)

    def send_near_last(self, d):
        landed(self.via_last.at[d], self.via_last_sem.at[d])
        rows = self.rows(1 - d)
        mine = self.part[1 + d, rows].astype(F32)
        self.part[1 + d, rows] = (mine + self.via_last[d].astype(F32)).astype(BF16)
        target = self.device(self.first, self.second + NEAR[d][1])
        self.send(self.part.at[1 + d], self.near_last.at[d], self.near_last_sem.at[d], target)

    def last(self, out_ref):
        for d in (0, 1):
            landed(self.near_last.at[d], self.near_last_sem.at[d])
        mine = self.total(3)
        out_ref[...] = mine + self.near_last[0].astype(F32) + self.near_last[1].astype(F32)


class Exchange:
    def __init__(self, count, send, recv, send_sem, recv_sem):
        self.count = count
        self.send, self.recv = send, recv
        self.send_sem, self.recv_sem = send_sem, recv_sem
        self.ep, self.rep = lax.axis_index("ep"), lax.axis_index("rep")

    def copy(self, other, place):
        return pltpu.make_async_remote_copy(
            src_ref=self.send.at[other],
            dst_ref=self.recv.at[place],
            send_sem=self.send_sem.at[0],
            recv_sem=self.recv_sem.at[0],
            device_id=(other, self.rep),
            device_id_type=MESH,
        )

    def each(self, body):
        def run(i, carry):
            body(lax.rem(self.ep + i, self.count))
            return carry

        lax.fori_loop(1, self.count, run, 0)

    def start(self):
        self.each(lambda other: self.copy(other, self.ep).start())
        self.recv[self.ep] = self.send[self.ep]

    def arrive(self):
        landed(self.recv.at[pl.ds(0, self.count - 1)], self.recv_sem.at[0])

    def finish(self):
        landed(self.send.at[pl.ds(0, self.count - 1)], self.send_sem.at[0])


def announce(count):
    ep, rep = lax.axis_index("ep"), lax.axis_index("rep")
    barrier = pltpu.get_barrier_semaphore()

    def run(i, carry):
        other = lax.rem(ep + i, count)
        pl.semaphore_signal(barrier, inc=1, device_id=(other, rep), device_id_type=MESH)
        return carry

    lax.fori_loop(1, count, run, 0)
    ring = Ring(True)
    for _, s in NEAR:
        for target in (ring.device(ring.first + s, ring.second), ring.device(ring.first, ring.second + s)):
            pl.semaphore_signal(barrier, inc=1, device_id=(ep, target), device_id_type=MESH)


def enter(count):
    pl.semaphore_wait(pltpu.get_barrier_semaphore(), count - 1 + 4)


def unpack(packed_ref, rows_ref):
    count, _, half = packed_ref.shape
    step = 4

    def run(i, carry):
        block = packed_ref[pl.ds(i * step, step)].astype(F32)
        at = pl.ds(pl.multiple_of(i * step * CAP, step * CAP), step * CAP)
        rows_ref[at, :half] = block[:, :CAP].reshape(step * CAP, half).astype(BF16)
        rows_ref[at, half:] = block[:, CAP:].reshape(step * CAP, half).astype(BF16)
        return carry

    lax.fori_loop(0, count // step, run, 0)


def pack(rows_ref, packed_ref):
    count, _, half = packed_ref.shape
    step = 4

    def run(i, carry):
        block = rows_ref[pl.ds(pl.multiple_of(i * step * CAP, step * CAP), step * CAP)]
        block = block.reshape(step, CAP, 2 * half)
        both = jnp.concatenate([block[:, :, :half], block[:, :, half:]], axis=1)
        packed_ref[pl.ds(i * step, step)] = both.astype(BF16)
        return carry

    lax.fori_loop(0, count // step, run, 0)


def weight_rows(weight_ref, j):
    pair = weight_ref[pl.ds(2 * j, 2)]
    return pair.reshape(2 * pair.shape[1], pair.shape[2])


def hidden_grads(slopes_in_ref, down_ref, wide_ref):
    unit = down_ref.shape[1]

    def run(j, carry):
        grads = contract_last(slopes_in_ref[...], weight_rows(down_ref, j))
        wide_ref[2 * j] = grads[:, :unit]
        wide_ref[2 * j + 1] = grads[:, unit:]
        return carry

    lax.fori_loop(0, down_ref.shape[0] // 2, run, 0)


def hidden_units(rows_ref, up_ref, wide_ref, hidden_ref, slopes_ref):
    unit = up_ref.shape[1]

    def run(j, carry):
        both = contract_last(rows_ref[...], weight_rows(up_ref, j))
        for i in range(2):
            pre = both[:, i * unit : (i + 1) * unit]
            slot = 2 * j + i
            other = lax.rem(slot, SIDE) * SIDE + lax.div(slot, SIDE)
            part = 0.5 * jnp.tanh(0.5 * pre) + 0.5
            value = pre * part
            slopes = wide_ref[other] * (part + value * (1.0 - part))
            at = pl.ds(pl.multiple_of(other * unit, unit), unit)
            hidden_ref[:, at] = value.astype(BF16)
            at = pl.ds(pl.multiple_of(slot * unit, unit), unit)
            slopes_ref[:, at] = slopes.astype(BF16)
        return carry

    lax.fori_loop(0, up_ref.shape[0] // 2, run, 0)


def project(left_ref, weight_ref, sum_ref):
    tile = 256

    def run(j, carry):
        at = pl.ds(pl.multiple_of(j * tile, tile), tile)
        right = weight_ref[:, :, at].reshape(-1, tile)
        sum_ref[:, at] = jnp.dot(left_ref[...], right, preferred_element_type=F32)
        return carry

    lax.fori_loop(0, sum_ref.shape[1] // tile, run, 0)


def weight_grads(scatter, step, left_ref, right_ref):
    unit = scatter.parts.shape[1]
    first = scatter.slot(scatter.first + step, 0)

    def run(i, carry):
        block = first + 2 * i
        left = left_ref[:, pl.ds(pl.multiple_of(block * unit, 2 * unit), 2 * unit)]
        grads = contract_first(left, right_ref[...]).astype(BF16)
        scatter.parts[pl.ds(block, 2)] = grads.reshape(2, unit, -1)
        return carry

    lax.fori_loop(0, SIDE // 2, run, 0)


def block_kernel(count, *refs):
    names = iter(refs)

    def take(n):
        return [next(names) for _ in range(n)]

    length, routes, gates = take(3)
    inputs, outputs = take(5), take(4)
    up_all, down_all = take(2)
    frames, kernel, cot = take(3)
    block_out, frame_grad, up_grad, down_grad = take(4)
    ranks, place, turned, mask, gate = take(5)
    normed, hat1, inv1, pad, conv, res, hat2, inv2 = take(8)
    send_slopes, send_rows, recv_slopes, recv_rows = take(4)
    back_out, back_grad, recv_out, recv_grad = take(4)
    slopes_in, rows_in, wide, hidden, slopes, row_sum = take(6)
    normed_grad, first_grad = take(2)
    up_parts, down_parts = take(2)
    up_room, down_room = take(5), take(5)
    in_sem, out_sem = take(2)
    exchange_sems = [take(2) for _ in range(4)]
    gather_sems = [take(5) for _ in range(2)]
    scatter_sems = [take(5) for _ in range(2)]

    gathers = [Gather(True, up_all, *gather_sems[0]), Gather(False, down_all, *gather_sems[1])]
    homes = (frames, kernel, up_all.at[gathers[0].here()], down_all.at[gathers[1].here()], cot)
    own = [pltpu.make_async_copy(a, b, in_sem.at[i]) for i, (a, b) in enumerate(zip(inputs, homes))]
    for i in (4, 2, 3, 0, 1):
        own[i].start()
    announce(count)

    def write(i, ref):
        copy = pltpu.make_async_copy(ref, outputs[i], out_sem.at[i])
        copy.start()
        written.append(copy)

    written = []
    to_slopes = Exchange(count, send_slopes, recv_slopes, *exchange_sems[0])
    to_rows = Exchange(count, send_rows, recv_rows, *exchange_sems[1])
    to_out = Exchange(count, back_out, recv_out, *exchange_sems[2])
    to_grad = Exchange(count, back_grad, recv_grad, *exchange_sems[3])
    scatters = [
        Scatter(True, up_parts, *up_room, *scatter_sems[0]),
        Scatter(False, down_parts, *down_room, *scatter_sems[1]),
    ]
    sides = [(slopes, rows_in), (hidden, slopes_in)]

    route_places(routes, ranks, place)
    live_columns(length, gates, mask, gate)
    own[4].wait()
    pack_slopes(cot, gate, place, send_slopes)
    enter(count)
    to_slopes.start()
    for i in (2, 3):
        own[i].wait()
    for gather in gathers:
        gather.start()
    for i in (0, 1):
        own[i].wait()
    front_norm(frames, mask, hat1, inv1, pad)
    depthwise(pad, kernel, conv, False)
    front_residual(frames, conv, res, hat2, inv2, normed)
    pack_rows(normed, place, send_rows)
    to_rows.start()

    for gather in gathers:
        gather.relay_near()
    for gather in gathers:
        gather.relay_row(0)
    for gather in gathers:
        gather.relay_far()
    for k in (1, 2, 3):
        for gather in gathers:
            gather.relay_row(k)
    turn_places(ranks, turned)
    to_slopes.arrive()
    unpack(recv_slopes, slopes_in)
    for k in range(SIDE):
        for gather in gathers:
            gather.end_row(k)
    hidden_grads(slopes_in, down_all, wide)
    to_rows.arrive()
    unpack(recv_rows, rows_in)
    hidden_units(rows_in, up_all, wide, hidden, slopes)
    project(slopes, up_all, row_sum)
    pack(row_sum, back_grad)
    to_grad.start()

    for scatter, (left, right) in zip(scatters, sides):
        weight_grads(scatter, 2, left, right)
        for i in range(SIDE):
            scatter.send_far(i)
    project(hidden, down_all, row_sum)
    pack(row_sum, back_out)
    to_out.start()
    for step in (1, -1):
        for scatter, (left, right) in zip(scatters, sides):
            weight_grads(scatter, step, left, right)
    for i in range(SIDE):
        for scatter in scatters:
            for d in (0, 1):
                scatter.send_near(d, i)
    for scatter, (left, right) in zip(scatters, sides):
        weight_grads(scatter, 0, left, right)
    for scatter in scatters:
        scatter.keep(0)
        scatter.send_far_last()
    for d in (0, 1):
        for scatter in scatters:
            scatter.keep(1 + d)
            scatter.send_near_last(d)

    to_grad.arrive()
    back_slopes(recv_grad, turned, normed_grad)
    back_residual(cot, hat2, inv2, conv, normed_grad, pad)
    depthwise(pad, kernel, first_grad, True)
    back_frames(first_grad, mask, hat1, inv1, normed_grad, frame_grad)
    write(1, frame_grad)
    for i, (scatter, out) in enumerate(zip(scatters, (up_grad, down_grad))):
        scatter.last(out)
        write(2 + i, out)
    to_out.arrive()
    back_mix(recv_out, turned, gate, res, block_out)
    write(0, block_out)

    for exchange in (to_slopes, to_rows, to_out, to_grad):
        exchange.finish()
    for ring, blocks in zip(gathers + scatters, (up_all, down_all, up_parts, down_parts)):
        ring.finish(blocks)
    for copy in written:
        copy.wait()


def hand_over(*refs):
    n = (len(refs) - 2) // 3
    inputs, outputs, rooms = refs[:n], refs[n : 2 * n], refs[2 * n : 3 * n]
    in_sem, out_sem = refs[3 * n :]
    reads = [pltpu.make_async_copy(inputs[i], rooms[i], in_sem.at[i]) for i in range(n)]
    writes = [pltpu.make_async_copy(rooms[i], outputs[i], out_sem.at[i]) for i in range(n)]
    for copy in reads:
        copy.start()
    for i in range(n):
        reads[i].wait()
        writes[i].start()
    for copy in writes:
        copy.wait()


def on_device(frames, lengths, routes, gate_weights, kernel, up_weight, down_weight, cotangent):
    experts = lax.axis_size("ep")
    reps = lax.axis_size("rep")
    count, width = frames.shape
    unit = up_weight.shape[1]
    rows = experts * CAP
    half = width // 2
    vmem = pltpu.VMEM
    packed = vmem((experts, 2 * CAP, half), BF16)
    grid32 = vmem((count, width), F32)
    column = vmem((count, 1), F32)
    weights = vmem((reps, unit, width), BF16)
    room = [
        vmem((2, SIDE, unit // 2, width), BF16),
        vmem((2, SIDE, unit, width), BF16),
        vmem((3, unit, width), BF16),
        vmem((2, unit // 2, width), BF16),
        vmem((2, unit, width), BF16),
    ]
    narrow = vmem((count, width), BF16)
    scratch = [weights, weights]
    scratch += [narrow, vmem(kernel.shape, F32), narrow]
    scratch += [narrow, narrow, vmem((unit, width), F32), vmem((unit, width), F32)]
    scratch += [vmem((2, count), F32), vmem((2 * rows, 4 * count), BF16)]
    scratch += [vmem((4, count, 2 * rows), BF16), column, vmem((2, count, 1), F32)]
    scratch += [narrow, grid32, column, vmem((count + 2 * EDGE, width), F32)]
    scratch += [grid32, grid32, grid32, column]
    scratch += [packed] * 8
    scratch += [vmem((rows, width), BF16)] * 2
    scratch += [vmem((reps, rows, unit), F32)]
    scratch += [vmem((rows, reps * unit), BF16)] * 2
    scratch += [vmem((rows, width), F32)]
    scratch += [grid32, grid32, weights, weights] + room + room
    scratch += [DMA((5,)), DMA((4,))]
    scratch += [DMA((1,))] * 8
    scratch += [DMA((1,)), DMA((2,)), DMA((2,)), DMA((2, SIDE)), DMA((2, SIDE))] * 2
    scratch += [DMA((1,)), DMA((2, SIDE)), DMA((2, SIDE)), DMA((2,)), DMA((2,))] * 2

    in_vmem = pl.BlockSpec(memory_space=pltpu.VMEM)
    anywhere = pl.BlockSpec(memory_space=pl.ANY)
    shapes = [jax.ShapeDtypeStruct((count, width), BF16)] * 2
    shapes += [jax.ShapeDtypeStruct((unit, width), F32)] * 2
    results = pl.pallas_call(
        functools.partial(block_kernel, experts),
        out_shape=shapes,
        in_specs=[in_vmem] * 3 + [anywhere] * 5,
        out_specs=[anywhere] * 4,
        scratch_shapes=scratch,
        compiler_params=pltpu.CompilerParams(
            collective_id=0, has_side_effects=True, vmem_limit_bytes=58 << 20
        ),
        cost_estimate=pl.CostEstimate(
            flops=12 * rows * reps * unit * width, bytes_accessed=8 << 20, transcendentals=0
        ),
    )(
        lengths.reshape(1, 1),
        routes.T,
        gate_weights.T,
        frames,
        kernel,
        up_weight[0],
        down_weight[0],
        cotangent,
    )
    block_out, frame_grad, up_grad, down_grad = pl.pallas_call(
        hand_over,
        out_shape=shapes,
        in_specs=[anywhere] * 4,
        out_specs=[anywhere] * 4,
        scratch_shapes=[vmem(s.shape, s.dtype) for s in shapes] + [DMA((4,)), DMA((4,))],
        compiler_params=pltpu.CompilerParams(vmem_limit_bytes=58 << 20),
    )(*results)
    return block_out, frame_grad, up_grad[None], down_grad[None]


def solution(mesh):
    in_specs = (
        P(("ep", "rep"), None),
        P(("ep", "rep")),
        P(("ep", "rep"), None),
        P(("ep", "rep"), None),
        P(),
        P("ep", "rep", None),
        P("ep", "rep", None),
        P(("ep", "rep"), None),
    )
    out_specs = (
        P(("ep", "rep"), None),
        P(("ep", "rep"), None),
        P("ep", "rep", None),
        P("ep", "rep", None),
    )
    return jax.shard_map(
        on_device, mesh=mesh, in_specs=in_specs, out_specs=out_specs, check_vma=False
    )
```

```python
import functools

import jax
import jax.numpy as jnp
from jax import lax
from jax.experimental import pallas as pl
from jax.experimental.pallas import tpu as pltpu
from jax.sharding import PartitionSpec as P

MESH = pl.DeviceIdType.MESH
DMA = pltpu.SemaphoreType.DMA
F32 = jnp.float32
BF16 = jnp.bfloat16

EPS = 1e-05
SIDE = 4
CAP = 8
TAPS = 31
EDGE = 16
NEAR = ((0, 1), (1, -1))
ORDER = (0, -1, 1, 2)
LEAVE = (2, 1, -1, 0)


def wrap(i, n):
    return lax.rem(i + n, n)


def lane_iota(shape):
    return lax.broadcasted_iota(jnp.int32, shape, 1)


def landed(ref, sem):
    pltpu.make_async_copy(ref, ref, sem).wait()


def to_column(row):
    count = row.shape[1]
    square = (count, count)
    here = lane_iota(square) == lax.broadcasted_iota(jnp.int32, square, 0)
    return jnp.sum(jnp.where(here, row, 0.0), axis=1, keepdims=True)


def route_places(routes_ref, rank_ref, place_ref):
    experts = place_ref.shape[0] // (2 * CAP)
    count = routes_ref.shape[1]
    shape = (experts, count)
    sub = lax.broadcasted_iota(jnp.int32, shape, 0)
    hot = [sub == routes_ref[k : k + 1] for k in range(2)]
    both = (hot[0].astype(F32) + hot[1].astype(F32)).astype(BF16)
    square = (count, count)
    earlier = lax.broadcasted_iota(jnp.int32, square, 0) < lane_iota(square)
    before = jnp.dot(both, earlier.astype(F32).astype(BF16), preferred_element_type=F32)
    tall = lax.broadcasted_iota(jnp.int32, (place_ref.shape[0], count), 0).astype(F32)
    for k in range(2):
        rank = jnp.sum(jnp.where(hot[k], before, 0.0), axis=0, keepdims=True)
        row = routes_ref[k : k + 1].astype(F32) * (2 * CAP) + rank
        rank_ref[k : k + 1] = row
        for h in range(2):
            at = slice((2 * k + h) * count, (2 * k + h + 1) * count)
            place_ref[:, at] = (tall == row + h * CAP).astype(F32).astype(BF16)


def turn_places(rank_ref, turned_ref):
    _, count, width = turned_ref.shape
    wide = lane_iota((count, width)).astype(F32)
    for k in range(2):
        row = to_column(rank_ref[k : k + 1])
        for h in range(2):
            turned_ref[2 * k + h] = (wide == row + h * CAP).astype(F32).astype(BF16)


def live_columns(length_ref, gates_ref, mask_ref, gate_ref):
    count = mask_ref.shape[0]
    positions = lax.broadcasted_iota(jnp.int32, (count, 1), 0)
    mask = (positions < length_ref[...]).astype(F32)
    mask_ref[...] = mask
    for k in range(2):
        gate_ref[k] = to_column(gates_ref[k : k + 1]) * mask


def contract_first(left, right):
    return lax.dot_general(left, right, (((0,), (0,)), ((), ())), preferred_element_type=F32)


def contract_last(left, right):
    return lax.dot_general(left, right, (((1,), (1,)), ((), ())), preferred_element_type=F32)


def pack_slopes(cot_ref, gate_ref, place_ref, out_ref):
    width = cot_ref.shape[1]
    half = width // 2
    cot = cot_ref[...].astype(F32)
    parts = []
    for k in range(2):
        scaled = (gate_ref[k] * cot).astype(BF16)
        parts += [scaled[:, :half], scaled[:, half:]]
    stacked = jnp.concatenate(parts, axis=0)
    packed = jnp.dot(place_ref[...], stacked, preferred_element_type=F32)
    out_ref[...] = packed.astype(BF16).reshape(out_ref.shape)


def pack_rows(normed_ref, place_ref, out_ref):
    width = normed_ref.shape[1]
    half = width // 2
    stacked = jnp.concatenate([normed_ref[:, :half], normed_ref[:, half:]], axis=0)
    middle = place_ref.shape[1] // 2
    place = place_ref[:, :middle] + place_ref[:, middle:]
    packed = jnp.dot(place, stacked, preferred_element_type=F32)
    out_ref[...] = packed.astype(BF16).reshape(out_ref.shape)


def over_rows(count, step, body):
    def run(i, carry):
        body(pl.ds(pl.multiple_of(i * step, step), step), pl.multiple_of(i * step, step))
        return carry

    lax.fori_loop(0, count // step, run, 0)


def normalize(values):
    center = values - jnp.mean(values, axis=-1, keepdims=True)
    inverse = lax.rsqrt(jnp.mean(center * center, axis=-1, keepdims=True) + EPS)
    return center * inverse, inverse


def norm_back(normed, inverse, upstream):
    mean_grad = jnp.mean(upstream, axis=-1, keepdims=True)
    mean_cross = jnp.mean(upstream * normed, axis=-1, keepdims=True)
    return inverse * (upstream - mean_grad - normed * mean_cross)


def silu_slope(values):
    part = jax.nn.sigmoid(values)
    return part + values * part * (1.0 - part)


def depthwise(pad_ref, kernel_ref, out_ref, reverse):
    count, width = out_ref.shape
    columns = 128

    def run(i, carry):
        at = pl.ds(pl.multiple_of(i * columns, columns), columns)
        total = jnp.zeros((count, columns), F32)
        for shift in range(8):
            part = None
            for base in range(0, 32, 8):
                j = base + shift - 1
                if j < 0 or j >= TAPS:
                    continue
                row = TAPS - 1 - j if reverse else j
                term = kernel_ref[row : row + 1, at] * pad_ref[base : base + count + 8, at]
                part = term if part is None else part + term
            if shift:
                part = pltpu.roll(part, count + 8 - shift, 0)
            total = total + part[:count]
        out_ref[:, at] = total
        return carry

    lax.fori_loop(0, width // columns, run, 0)


def front_norm(frames_ref, mask_ref, hat_ref, inv_ref, pad_ref):
    count, width = frames_ref.shape
    pad_ref[:EDGE] = jnp.zeros((EDGE, width), F32)
    pad_ref[EDGE + count :] = jnp.zeros((EDGE, width), F32)

    def body(at, start):
        hat, inverse = normalize(frames_ref[at].astype(F32))
        hat_ref[at] = hat
        inv_ref[at] = inverse
        pad_ref[pl.ds(start + EDGE, 16)] = hat * mask_ref[at]

    over_rows(count, 16, body)


def front_residual(frames_ref, conv_ref, res_ref, hat_ref, inv_ref, normed_ref):
    def body(at, start):
        residual = frames_ref[at].astype(F32) + jax.nn.silu(conv_ref[at])
        hat, inverse = normalize(residual)
        res_ref[at] = residual
        hat_ref[at] = hat
        inv_ref[at] = inverse
        normed_ref[at] = hat.astype(BF16)

    over_rows(frames_ref.shape[0], 16, body)


def back_mix(back_ref, place_ref, gate_ref, res_ref, out_ref):
    half = back_ref.shape[2]
    rows = back_ref[...].reshape(-1, half)
    for h in range(2):
        at = slice(h * half, (h + 1) * half)
        mixed = gate_ref[0] * jnp.dot(place_ref[h], rows, preferred_element_type=F32)
        mixed += gate_ref[1] * jnp.dot(place_ref[2 + h], rows, preferred_element_type=F32)
        out_ref[:, at] = (res_ref[:, at] + mixed).astype(BF16)


def back_slopes(back_ref, place_ref, grad_ref):
    half = back_ref.shape[2]
    rows = back_ref[...].reshape(-1, half)
    for h in range(2):
        pick = place_ref[h] + place_ref[2 + h]
        grad_ref[:, h * half : (h + 1) * half] = jnp.dot(pick, rows, preferred_element_type=F32)


def back_residual(cot_ref, hat_ref, inv_ref, conv_ref, grad_ref, pad_ref):
    def body(at, start):
        grad = cot_ref[at].astype(F32) + norm_back(hat_ref[at], inv_ref[at], grad_ref[at])
        grad_ref[at] = grad
        pad_ref[pl.ds(start + EDGE, 16)] = grad * silu_slope(conv_ref[at])

    over_rows(cot_ref.shape[0], 16, body)


def back_frames(first_ref, mask_ref, hat_ref, inv_ref, grad_ref, out_ref):
    def body(at, start):
        first = first_ref[at] * mask_ref[at]
        out_ref[at] = (grad_ref[at] + norm_back(hat_ref[at], inv_ref[at], first)).astype(BF16)

    over_rows(out_ref.shape[0], 16, body)


class Ring:
    def __init__(self, x_first):
        rep = lax.axis_index("rep")
        x, y = lax.rem(rep, SIDE), lax.div(rep, SIDE)
        self.x_first = x_first
        self.ep = lax.axis_index("ep")
        self.first, self.second = (x, y) if x_first else (y, x)

    def device(self, first, second):
        first, second = wrap(first, SIDE), wrap(second, SIDE)
        return second * SIDE + first if self.x_first else first * SIDE + second

    def here(self):
        return self.slot(self.first, self.second)

    def slot(self, first, second):
        return wrap(first, SIDE) * SIDE + wrap(second, SIDE)

    def send(self, src, dst, recv_sem, target):
        pltpu.make_async_remote_copy(
            src_ref=src,
            dst_ref=dst,
            send_sem=self.send_sem.at[0],
            recv_sem=recv_sem,
            device_id=(self.ep, target),
            device_id_type=MESH,
        ).start()

    def finish(self, blocks):
        landed(blocks.at[pl.ds(0, SIDE * SIDE - 1)], self.send_sem.at[0])


class Gather(Ring):
    def __init__(self, x_first, full, send_sem, near_sem, far_sem, row_sem, row_far_sem):
        super().__init__(x_first)
        self.full, self.send_sem = full, send_sem
        self.near_sem, self.far_sem = near_sem, far_sem
        self.row_sem, self.row_far_sem = row_sem, row_far_sem
        self.half = full.shape[1] // 2

    def piece(self, block, half):
        if half is None:
            return self.full.at[block]
        return self.full.at[block, pl.ds(half * self.half, self.half)]

    def push(self, block, half, target, sem):
        ref = self.piece(block, half)
        self.send(ref, ref, sem, target)

    def start(self):
        block = self.here()
        for d, s in NEAR:
            self.push(block, None, self.device(self.first + s, self.second), self.near_sem.at[d])
        self.across(0)

    def across(self, k):
        block = self.slot(self.first + ORDER[k], self.second)
        for d, s in NEAR:
            target = self.device(self.first, self.second + s)
            self.push(block, None, target, self.row_sem.at[d, k])

    def relay_near(self):
        for d, s in NEAR:
            block = self.slot(self.first - s, self.second)
            landed(self.piece(block, None), self.near_sem.at[d])
            self.push(block, d, self.device(self.first + s, self.second), self.far_sem.at[d])
            self.across(1 + d)

    def relay_far(self):
        block = self.slot(self.first + 2, self.second)
        for d in (0, 1):
            landed(self.piece(block, d), self.far_sem.at[d])
        self.across(3)

    def relay_row(self, k):
        for d, s in NEAR:
            block = self.slot(self.first + ORDER[k], self.second - s)
            landed(self.piece(block, None), self.row_sem.at[d, k])
            target = self.device(self.first, self.second + s)
            self.push(block, d, target, self.row_far_sem.at[d, k])

    def end_row(self, k):
        block = self.slot(self.first + ORDER[k], self.second + 2)
        for d in (0, 1):
            landed(self.piece(block, d), self.row_far_sem.at[d, k])


class Scatter(Ring):
    def __init__(self, x_first, parts, via, near, part, via_last, near_last, send_sem, *sems):
        super().__init__(x_first)
        self.parts, self.via, self.near, self.part = parts, via, near, part
        self.via_last, self.near_last = via_last, near_last
        self.send_sem = send_sem
        self.via_sem, self.near_sem, self.via_last_sem, self.near_last_sem = sems
        self.half = parts.shape[1] // 2

    def rows(self, half):
        return pl.ds(half * self.half, self.half)

    def block(self, step, i):
        return self.slot(self.first + step, self.second + LEAVE[i])

    def send_far(self, i):
        block = self.block(2, i)
        for d, s in NEAR:
            target = self.device(self.first + s, self.second)
            src = self.parts.at[block, self.rows(1 - d)]
            self.send(src, self.via.at[d, i], self.via_sem.at[d, i], target)

    def send_near(self, d, i):
        s = NEAR[d][1]
        block = self.block(s, i)
        landed(self.via.at[d, i], self.via_sem.at[d, i])
        rows = self.rows(1 - d)
        mine = self.parts[block, rows].astype(F32)
        self.parts[block, rows] = (mine + self.via[d, i].astype(F32)).astype(BF16)
        target = self.device(self.first + s, self.second)
        self.send(self.parts.at[block], self.near.at[d, i], self.near_sem.at[d, i], target)

    def total(self, i):
        for d in (0, 1):
            landed(self.near.at[d, i], self.near_sem.at[d, i])
        mine = self.parts[self.block(0, i)].astype(F32)
        return mine + self.near[0, i].astype(F32) + self.near[1, i].astype(F32)

    def keep(self, i):
        self.part[i] = self.total(i).astype(BF16)

    def send_far_last(self):
        for d, s in NEAR:
            target = self.device(self.first, self.second + s)
            src = self.part.at[0, self.rows(1 - d)]
            self.send(src, self.via_last.at[d], self.via_last_sem.at[d], target)

    def send_near_last(self, d):
        landed(self.via_last.at[d], self.via_last_sem.at[d])
        rows = self.rows(1 - d)
        mine = self.part[1 + d, rows].astype(F32)
        self.part[1 + d, rows] = (mine + self.via_last[d].astype(F32)).astype(BF16)
        target = self.device(self.first, self.second + NEAR[d][1])
        self.send(self.part.at[1 + d], self.near_last.at[d], self.near_last_sem.at[d], target)

    def last(self, out_ref):
        for d in (0, 1):
            landed(self.near_last.at[d], self.near_last_sem.at[d])
        mine = self.total(3)
        out_ref[...] = mine + self.near_last[0].astype(F32) + self.near_last[1].astype(F32)


class Exchange:
    def __init__(self, count, send, recv, send_sem, recv_sem):
        self.count = count
        self.send, self.recv = send, recv
        self.send_sem, self.recv_sem = send_sem, recv_sem
        self.ep, self.rep = lax.axis_index("ep"), lax.axis_index("rep")

    def copy(self, other, place):
        return pltpu.make_async_remote_copy(
            src_ref=self.send.at[other],
            dst_ref=self.recv.at[place],
            send_sem=self.send_sem.at[0],
            recv_sem=self.recv_sem.at[0],
            device_id=(other, self.rep),
            device_id_type=MESH,
        )

    def each(self, body):
        def run(i, carry):
            body(lax.rem(self.ep + i, self.count))
            return carry

        lax.fori_loop(1, self.count, run, 0)

    def start(self):
        self.each(lambda other: self.copy(other, self.ep).start())
        self.recv[self.ep] = self.send[self.ep]

    def arrive(self):
        landed(self.recv.at[pl.ds(0, self.count - 1)], self.recv_sem.at[0])

    def finish(self):
        landed(self.send.at[pl.ds(0, self.count - 1)], self.send_sem.at[0])


def announce(count):
    ep, rep = lax.axis_index("ep"), lax.axis_index("rep")
    barrier = pltpu.get_barrier_semaphore()

    def run(i, carry):
        other = lax.rem(ep + i, count)
        pl.semaphore_signal(barrier, inc=1, device_id=(other, rep), device_id_type=MESH)
        return carry

    lax.fori_loop(1, count, run, 0)
    ring = Ring(True)
    for _, s in NEAR:
        for target in (ring.device(ring.first + s, ring.second), ring.device(ring.first, ring.second + s)):
            pl.semaphore_signal(barrier, inc=1, device_id=(ep, target), device_id_type=MESH)


def enter(count):
    pl.semaphore_wait(pltpu.get_barrier_semaphore(), count - 1 + 4)


def unpack(packed_ref, rows_ref):
    count, _, half = packed_ref.shape
    step = 4

    def run(i, carry):
        block = packed_ref[pl.ds(i * step, step)].astype(F32)
        at = pl.ds(pl.multiple_of(i * step * CAP, step * CAP), step * CAP)
        rows_ref[at, :half] = block[:, :CAP].reshape(step * CAP, half).astype(BF16)
        rows_ref[at, half:] = block[:, CAP:].reshape(step * CAP, half).astype(BF16)
        return carry

    lax.fori_loop(0, count // step, run, 0)


def pack(rows_ref, packed_ref):
    count, _, half = packed_ref.shape
    step = 4

    def run(i, carry):
        block = rows_ref[pl.ds(pl.multiple_of(i * step * CAP, step * CAP), step * CAP)]
        block = block.reshape(step, CAP, 2 * half)
        both = jnp.concatenate([block[:, :, :half], block[:, :, half:]], axis=1)
        packed_ref[pl.ds(i * step, step)] = both.astype(BF16)
        return carry

    lax.fori_loop(0, count // step, run, 0)


def weight_rows(weight_ref, j):
    pair = weight_ref[pl.ds(2 * j, 2)]
    return pair.reshape(2 * pair.shape[1], pair.shape[2])


def hidden_grads(slopes_in_ref, down_ref, wide_ref, side):
    unit = down_ref.shape[1]

    def run(i, carry):
        j = (SIDE // 2) * i + side
        grads = contract_last(slopes_in_ref[...], weight_rows(down_ref, j))
        wide_ref[2 * j] = grads[:, :unit]
        wide_ref[2 * j + 1] = grads[:, unit:]
        return carry

    lax.fori_loop(0, SIDE, run, 0, unroll=True)


def hidden_units(rows_ref, up_ref, wide_ref, hidden_ref, slopes_ref):
    unit = up_ref.shape[1]

    def run(j, carry):
        both = contract_last(rows_ref[...], weight_rows(up_ref, j))
        for i in range(2):
            pre = both[:, i * unit : (i + 1) * unit]
            slot = 2 * j + i
            other = lax.rem(slot, SIDE) * SIDE + lax.div(slot, SIDE)
            part = 0.5 * jnp.tanh(0.5 * pre) + 0.5
            value = pre * part
            slopes = wide_ref[other] * (part + value * (1.0 - part))
            at = pl.ds(pl.multiple_of(other * unit, unit), unit)
            hidden_ref[:, at] = value.astype(BF16)
            at = pl.ds(pl.multiple_of(slot * unit, unit), unit)
            slopes_ref[:, at] = slopes.astype(BF16)
        return carry

    lax.fori_loop(0, up_ref.shape[0] // 2, run, 0, unroll=True)


def project(left_ref, weight_ref, sum_ref):
    tile = 256

    def run(j, carry):
        at = pl.ds(pl.multiple_of(j * tile, tile), tile)
        right = weight_ref[:, :, at].reshape(-1, tile)
        sum_ref[:, at] = jnp.dot(left_ref[...], right, preferred_element_type=F32)
        return carry

    lax.fori_loop(0, sum_ref.shape[1] // tile, run, 0, unroll=True)


def weight_grads(scatter, step, left_ref, right_ref):
    unit = scatter.parts.shape[1]
    first = scatter.slot(scatter.first + step, 0)

    def run(i, carry):
        block = first + 2 * i
        left = left_ref[:, pl.ds(pl.multiple_of(block * unit, 2 * unit), 2 * unit)]
        grads = contract_first(left, right_ref[...]).astype(BF16)
        scatter.parts[pl.ds(block, 2)] = grads.reshape(2, unit, -1)
        return carry

    lax.fori_loop(0, SIDE // 2, run, 0, unroll=True)


def block_kernel(count, *refs):
    names = iter(refs)

    def take(n):
        return [next(names) for _ in range(n)]

    length, routes, gates = take(3)
    inputs, outputs = take(5), take(4)
    up_all, down_all = take(2)
    frames, kernel, cot = take(3)
    block_out, frame_grad, up_grad, down_grad = take(4)
    ranks, place, turned, mask, gate = take(5)
    normed, hat1, inv1, pad, conv, res, hat2, inv2 = take(8)
    send_slopes, send_rows, recv_slopes, recv_rows = take(4)
    back_out, back_grad, recv_out, recv_grad = take(4)
    slopes_in, rows_in, wide, hidden, slopes, row_sum = take(6)
    normed_grad, first_grad = take(2)
    up_parts, down_parts = take(2)
    up_room, down_room = take(5), take(5)
    in_sem, out_sem = take(2)
    exchange_sems = [take(2) for _ in range(4)]
    gather_sems = [take(5) for _ in range(2)]
    scatter_sems = [take(5) for _ in range(2)]

    gathers = [Gather(True, up_all, *gather_sems[0]), Gather(False, down_all, *gather_sems[1])]
    homes = (frames, kernel, up_all.at[gathers[0].here()], down_all.at[gathers[1].here()], cot)
    own = [pltpu.make_async_copy(a, b, in_sem.at[i]) for i, (a, b) in enumerate(zip(inputs, homes))]
    for i in (4, 2, 3, 0, 1):
        own[i].start()
    announce(count)

    def write(i, ref):
        copy = pltpu.make_async_copy(ref, outputs[i], out_sem.at[i])
        copy.start()
        written.append(copy)

    written = []
    to_slopes = Exchange(count, send_slopes, recv_slopes, *exchange_sems[0])
    to_rows = Exchange(count, send_rows, recv_rows, *exchange_sems[1])
    to_out = Exchange(count, back_out, recv_out, *exchange_sems[2])
    to_grad = Exchange(count, back_grad, recv_grad, *exchange_sems[3])
    scatters = [
        Scatter(True, up_parts, *up_room, *scatter_sems[0]),
        Scatter(False, down_parts, *down_room, *scatter_sems[1]),
    ]
    sides = [(slopes, rows_in), (hidden, slopes_in)]

    route_places(routes, ranks, place)
    live_columns(length, gates, mask, gate)
    own[4].wait()
    pack_slopes(cot, gate, place, send_slopes)
    enter(count)
    to_slopes.start()
    for i in (2, 3):
        own[i].wait()
    for gather in gathers:
        gather.start()
    for i in (0, 1):
        own[i].wait()
    front_norm(frames, mask, hat1, inv1, pad)
    depthwise(pad, kernel, conv, False)
    front_residual(frames, conv, res, hat2, inv2, normed)
    pack_rows(normed, place, send_rows)
    to_rows.start()

    for gather in gathers:
        gather.relay_near()
    for gather in gathers:
        gather.relay_row(0)
    for gather in gathers:
        gather.relay_far()
    for k in (1, 2, 3):
        for gather in gathers:
            gather.relay_row(k)
    turn_places(ranks, turned)
    to_slopes.arrive()
    unpack(recv_slopes, slopes_in)
    near_side = lax.div(gathers[1].second, SIDE // 2)
    hidden_grads(slopes_in, down_all, wide, near_side)
    for k in range(SIDE):
        for gather in gathers:
            gather.end_row(k)
    hidden_grads(slopes_in, down_all, wide, 1 - near_side)
    to_rows.arrive()
    unpack(recv_rows, rows_in)
    hidden_units(rows_in, up_all, wide, hidden, slopes)
    project(slopes, up_all, row_sum)
    pack(row_sum, back_grad)
    to_grad.start()

    def each(step):
        for scatter in scatters:
            step(scatter)

    def both_near(i):
        for d in (0, 1):
            each(lambda scatter: scatter.send_near(d, i))

    def all_grads(step):
        for scatter, (left, right) in zip(scatters, sides):
            weight_grads(scatter, step, left, right)

    all_grads(2)
    each(lambda scatter: scatter.send_far(0))
    each(lambda scatter: scatter.send_far(1))
    project(hidden, down_all, row_sum)
    pack(row_sum, back_out)
    to_out.start()
    all_grads(1)
    all_grads(-1)
    each(lambda scatter: scatter.send_far(2))
    both_near(0)
    each(lambda scatter: scatter.send_far(3))
    both_near(1)
    all_grads(0)
    both_near(2)
    each(lambda scatter: scatter.keep(0))
    each(lambda scatter: scatter.send_far_last())
    both_near(3)
    for d in (0, 1):
        each(lambda scatter: scatter.keep(1 + d))
        each(lambda scatter: scatter.send_near_last(d))

    to_grad.arrive()
    back_slopes(recv_grad, turned, normed_grad)
    back_residual(cot, hat2, inv2, conv, normed_grad, pad)
    depthwise(pad, kernel, first_grad, True)
    back_frames(first_grad, mask, hat1, inv1, normed_grad, frame_grad)
    write(1, frame_grad)
    for i, (scatter, out) in enumerate(zip(scatters, (up_grad, down_grad))):
        scatter.last(out)
        write(2 + i, out)
    to_out.arrive()
    back_mix(recv_out, turned, gate, res, block_out)
    write(0, block_out)

    for exchange in (to_slopes, to_rows, to_out, to_grad):
        exchange.finish()
    for ring, blocks in zip(gathers + scatters, (up_all, down_all, up_parts, down_parts)):
        ring.finish(blocks)
    for copy in written:
        copy.wait()


def hand_over(*refs):
    n = (len(refs) - 2) // 3
    inputs, outputs, rooms = refs[:n], refs[n : 2 * n], refs[2 * n : 3 * n]
    in_sem, out_sem = refs[3 * n :]
    reads = [pltpu.make_async_copy(inputs[i], rooms[i], in_sem.at[i]) for i in range(n)]
    writes = [pltpu.make_async_copy(rooms[i], outputs[i], out_sem.at[i]) for i in range(n)]
    for copy in reads:
        copy.start()
    for i in range(n):
        reads[i].wait()
        writes[i].start()
    for copy in writes:
        copy.wait()


def on_device(frames, lengths, routes, gate_weights, kernel, up_weight, down_weight, cotangent):
    experts = lax.axis_size("ep")
    reps = lax.axis_size("rep")
    count, width = frames.shape
    unit = up_weight.shape[1]
    rows = experts * CAP
    half = width // 2
    vmem = pltpu.VMEM
    packed = vmem((experts, 2 * CAP, half), BF16)
    grid32 = vmem((count, width), F32)
    column = vmem((count, 1), F32)
    weights = vmem((reps, unit, width), BF16)
    room = [
        vmem((2, SIDE, unit // 2, width), BF16),
        vmem((2, SIDE, unit, width), BF16),
        vmem((3, unit, width), BF16),
        vmem((2, unit // 2, width), BF16),
        vmem((2, unit, width), BF16),
    ]
    narrow = vmem((count, width), BF16)
    scratch = [weights, weights]
    scratch += [narrow, vmem(kernel.shape, F32), narrow]
    scratch += [narrow, narrow, vmem((unit, width), F32), vmem((unit, width), F32)]
    scratch += [vmem((2, count), F32), vmem((2 * rows, 4 * count), BF16)]
    scratch += [vmem((4, count, 2 * rows), BF16), column, vmem((2, count, 1), F32)]
    scratch += [narrow, grid32, column, vmem((count + 2 * EDGE, width), F32)]
    scratch += [grid32, grid32, grid32, column]
    scratch += [packed] * 8
    scratch += [vmem((rows, width), BF16)] * 2
    scratch += [vmem((reps, rows, unit), F32)]
    scratch += [vmem((rows, reps * unit), BF16)] * 2
    scratch += [vmem((rows, width), F32)]
    scratch += [grid32, grid32, weights, weights] + room + room
    scratch += [DMA((5,)), DMA((4,))]
    scratch += [DMA((1,))] * 8
    scratch += [DMA((1,)), DMA((2,)), DMA((2,)), DMA((2, SIDE)), DMA((2, SIDE))] * 2
    scratch += [DMA((1,)), DMA((2, SIDE)), DMA((2, SIDE)), DMA((2,)), DMA((2,))] * 2

    in_vmem = pl.BlockSpec(memory_space=pltpu.VMEM)
    anywhere = pl.BlockSpec(memory_space=pl.ANY)
    shapes = [jax.ShapeDtypeStruct((count, width), BF16)] * 2
    shapes += [jax.ShapeDtypeStruct((unit, width), F32)] * 2
    results = pl.pallas_call(
        functools.partial(block_kernel, experts),
        out_shape=shapes,
        in_specs=[in_vmem] * 3 + [anywhere] * 5,
        out_specs=[anywhere] * 4,
        scratch_shapes=scratch,
        compiler_params=pltpu.CompilerParams(
            collective_id=0, has_side_effects=True, vmem_limit_bytes=58 << 20
        ),
        cost_estimate=pl.CostEstimate(
            flops=12 * rows * reps * unit * width, bytes_accessed=8 << 20, transcendentals=0
        ),
    )(
        lengths.reshape(1, 1),
        routes.T,
        gate_weights.T,
        frames,
        kernel,
        up_weight[0],
        down_weight[0],
        cotangent,
    )
    block_out, frame_grad, up_grad, down_grad = pl.pallas_call(
        hand_over,
        out_shape=shapes,
        in_specs=[anywhere] * 4,
        out_specs=[anywhere] * 4,
        scratch_shapes=[vmem(s.shape, s.dtype) for s in shapes] + [DMA((4,)), DMA((4,))],
        compiler_params=pltpu.CompilerParams(vmem_limit_bytes=58 << 20),
    )(*results)
    return block_out, frame_grad, up_grad[None], down_grad[None]


def solution(mesh):
    in_specs = (
        P(("ep", "rep"), None),
        P(("ep", "rep")),
        P(("ep", "rep"), None),
        P(("ep", "rep"), None),
        P(),
        P("ep", "rep", None),
        P("ep", "rep", None),
        P(("ep", "rep"), None),
    )
    out_specs = (
        P(("ep", "rep"), None),
        P(("ep", "rep"), None),
        P("ep", "rep", None),
        P("ep", "rep", None),
    )
    return jax.shard_map(
        on_device, mesh=mesh, in_specs=in_specs, out_specs=out_specs, check_vma=False
    )
```

```python
import functools

import jax
import jax.numpy as jnp
from jax import lax
from jax.experimental import pallas as pl
from jax.experimental.pallas import tpu as pltpu
from jax.sharding import PartitionSpec as P

MESH = pl.DeviceIdType.MESH
DMA = pltpu.SemaphoreType.DMA
F32 = jnp.float32
BF16 = jnp.bfloat16

EPS = 1e-05
SIDE = 4
CAP = 8
TAPS = 31
EDGE = 16
NEAR = ((0, 1), (1, -1))
ORDER = (0, -1, 1, 2)
LEAVE = (2, 1, -1, 0)


def wrap(i, n):
    return lax.rem(i + n, n)


def lane_iota(shape):
    return lax.broadcasted_iota(jnp.int32, shape, 1)


def landed(ref, sem):
    pltpu.make_async_copy(ref, ref, sem).wait()


def to_column(row):
    count = row.shape[1]
    square = (count, count)
    here = lane_iota(square) == lax.broadcasted_iota(jnp.int32, square, 0)
    return jnp.sum(jnp.where(here, row, 0.0), axis=1, keepdims=True)


def route_places(routes_ref, rank_ref, place_ref):
    experts = place_ref.shape[0] // (2 * CAP)
    count = routes_ref.shape[1]
    shape = (experts, count)
    sub = lax.broadcasted_iota(jnp.int32, shape, 0)
    hot = [sub == routes_ref[k : k + 1] for k in range(2)]
    both = (hot[0].astype(F32) + hot[1].astype(F32)).astype(BF16)
    square = (count, count)
    earlier = lax.broadcasted_iota(jnp.int32, square, 0) < lane_iota(square)
    before = jnp.dot(both, earlier.astype(F32).astype(BF16), preferred_element_type=F32)
    tall = lax.broadcasted_iota(jnp.int32, (place_ref.shape[0], count), 0).astype(F32)
    for k in range(2):
        rank = jnp.sum(jnp.where(hot[k], before, 0.0), axis=0, keepdims=True)
        row = routes_ref[k : k + 1].astype(F32) * (2 * CAP) + rank
        rank_ref[k : k + 1] = row
        for h in range(2):
            at = slice((2 * k + h) * count, (2 * k + h + 1) * count)
            place_ref[:, at] = (tall == row + h * CAP).astype(F32).astype(BF16)


def turn_places(rank_ref, turned_ref):
    _, count, width = turned_ref.shape
    wide = lane_iota((count, width)).astype(F32)
    for k in range(2):
        row = to_column(rank_ref[k : k + 1])
        for h in range(2):
            turned_ref[2 * k + h] = (wide == row + h * CAP).astype(F32).astype(BF16)


def live_columns(length_ref, gates_ref, mask_ref, gate_ref):
    count = mask_ref.shape[0]
    positions = lax.broadcasted_iota(jnp.int32, (count, 1), 0)
    mask = (positions < length_ref[...]).astype(F32)
    mask_ref[...] = mask
    for k in range(2):
        gate_ref[k] = to_column(gates_ref[k : k + 1]) * mask


def contract_first(left, right):
    return lax.dot_general(left, right, (((0,), (0,)), ((), ())), preferred_element_type=F32)


def contract_last(left, right):
    return lax.dot_general(left, right, (((1,), (1,)), ((), ())), preferred_element_type=F32)


def pack_slopes(cot_ref, gate_ref, place_ref, out_ref):
    width = cot_ref.shape[1]
    half = width // 2
    cot = cot_ref[...].astype(F32)
    parts = []
    for k in range(2):
        scaled = (gate_ref[k] * cot).astype(BF16)
        parts += [scaled[:, :half], scaled[:, half:]]
    stacked = jnp.concatenate(parts, axis=0)
    packed = jnp.dot(place_ref[...], stacked, preferred_element_type=F32)
    out_ref[...] = packed.astype(BF16).reshape(out_ref.shape)


def pack_rows(normed_ref, place_ref, out_ref):
    width = normed_ref.shape[1]
    half = width // 2
    stacked = jnp.concatenate([normed_ref[:, :half], normed_ref[:, half:]], axis=0)
    middle = place_ref.shape[1] // 2
    place = place_ref[:, :middle] + place_ref[:, middle:]
    packed = jnp.dot(place, stacked, preferred_element_type=F32)
    out_ref[...] = packed.astype(BF16).reshape(out_ref.shape)


def over_rows(count, step, body):
    def run(i, carry):
        body(pl.ds(pl.multiple_of(i * step, step), step), pl.multiple_of(i * step, step))
        return carry

    lax.fori_loop(0, count // step, run, 0)


def normalize(values):
    center = values - jnp.mean(values, axis=-1, keepdims=True)
    inverse = lax.rsqrt(jnp.mean(center * center, axis=-1, keepdims=True) + EPS)
    return center * inverse, inverse


def norm_back(normed, inverse, upstream):
    mean_grad = jnp.mean(upstream, axis=-1, keepdims=True)
    mean_cross = jnp.mean(upstream * normed, axis=-1, keepdims=True)
    return inverse * (upstream - mean_grad - normed * mean_cross)


def silu_slope(values):
    part = jax.nn.sigmoid(values)
    return part + values * part * (1.0 - part)


def depthwise(pad_ref, kernel_ref, out_ref, reverse):
    count, width = out_ref.shape
    columns = 128

    def run(i, carry):
        at = pl.ds(pl.multiple_of(i * columns, columns), columns)
        total = jnp.zeros((count, columns), F32)
        for shift in range(8):
            part = None
            for base in range(0, 32, 8):
                j = base + shift - 1
                if j < 0 or j >= TAPS:
                    continue
                row = TAPS - 1 - j if reverse else j
                term = kernel_ref[row : row + 1, at] * pad_ref[base : base + count + 8, at]
                part = term if part is None else part + term
            if shift:
                part = pltpu.roll(part, count + 8 - shift, 0)
            total = total + part[:count]
        out_ref[:, at] = total
        return carry

    lax.fori_loop(0, width // columns, run, 0)


def front_norm(frames_ref, mask_ref, hat_ref, inv_ref, pad_ref):
    count, width = frames_ref.shape
    pad_ref[:EDGE] = jnp.zeros((EDGE, width), F32)
    pad_ref[EDGE + count :] = jnp.zeros((EDGE, width), F32)

    def body(at, start):
        hat, inverse = normalize(frames_ref[at].astype(F32))
        hat_ref[at] = hat
        inv_ref[at] = inverse
        pad_ref[pl.ds(start + EDGE, 16)] = hat * mask_ref[at]

    over_rows(count, 16, body)


def front_residual(frames_ref, conv_ref, res_ref, hat_ref, inv_ref, normed_ref):
    def body(at, start):
        residual = frames_ref[at].astype(F32) + jax.nn.silu(conv_ref[at])
        hat, inverse = normalize(residual)
        res_ref[at] = residual
        hat_ref[at] = hat
        inv_ref[at] = inverse
        normed_ref[at] = hat.astype(BF16)

    over_rows(frames_ref.shape[0], 16, body)


def back_mix(back_ref, place_ref, gate_ref, res_ref, out_ref):
    half = back_ref.shape[2]
    rows = back_ref[...].reshape(-1, half)
    for h in range(2):
        at = slice(h * half, (h + 1) * half)
        mixed = gate_ref[0] * jnp.dot(place_ref[h], rows, preferred_element_type=F32)
        mixed += gate_ref[1] * jnp.dot(place_ref[2 + h], rows, preferred_element_type=F32)
        out_ref[:, at] = (res_ref[:, at] + mixed).astype(BF16)


def back_slopes(back_ref, place_ref, grad_ref):
    half = back_ref.shape[2]
    rows = back_ref[...].reshape(-1, half)
    for h in range(2):
        pick = place_ref[h] + place_ref[2 + h]
        grad_ref[:, h * half : (h + 1) * half] = jnp.dot(pick, rows, preferred_element_type=F32)


def back_residual(cot_ref, hat_ref, inv_ref, conv_ref, grad_ref, pad_ref):
    def body(at, start):
        grad = cot_ref[at].astype(F32) + norm_back(hat_ref[at], inv_ref[at], grad_ref[at])
        grad_ref[at] = grad
        pad_ref[pl.ds(start + EDGE, 16)] = grad * silu_slope(conv_ref[at])

    over_rows(cot_ref.shape[0], 16, body)


def back_frames(first_ref, mask_ref, hat_ref, inv_ref, grad_ref, out_ref):
    def body(at, start):
        first = first_ref[at] * mask_ref[at]
        out_ref[at] = (grad_ref[at] + norm_back(hat_ref[at], inv_ref[at], first)).astype(BF16)

    over_rows(out_ref.shape[0], 16, body)


class Ring:
    def __init__(self, x_first):
        rep = lax.axis_index("rep")
        x, y = lax.rem(rep, SIDE), lax.div(rep, SIDE)
        self.x_first = x_first
        self.ep = lax.axis_index("ep")
        self.first, self.second = (x, y) if x_first else (y, x)

    def device(self, first, second):
        first, second = wrap(first, SIDE), wrap(second, SIDE)
        return second * SIDE + first if self.x_first else first * SIDE + second

    def here(self):
        return self.slot(self.first, self.second)

    def slot(self, first, second):
        return wrap(first, SIDE) * SIDE + wrap(second, SIDE)

    def send(self, src, dst, recv_sem, target):
        pltpu.make_async_remote_copy(
            src_ref=src,
            dst_ref=dst,
            send_sem=self.send_sem.at[0],
            recv_sem=recv_sem,
            device_id=(self.ep, target),
            device_id_type=MESH,
        ).start()

    def finish(self, blocks):
        landed(blocks.at[pl.ds(0, SIDE * SIDE - 1)], self.send_sem.at[0])


class Gather(Ring):
    def __init__(self, x_first, full, send_sem, near_sem, far_sem, row_sem, row_far_sem):
        super().__init__(x_first)
        self.full, self.send_sem = full, send_sem
        self.near_sem, self.far_sem = near_sem, far_sem
        self.row_sem, self.row_far_sem = row_sem, row_far_sem
        self.half = full.shape[1] // 2

    def piece(self, block, half):
        if half is None:
            return self.full.at[block]
        return self.full.at[block, pl.ds(half * self.half, self.half)]

    def push(self, block, half, target, sem):
        ref = self.piece(block, half)
        self.send(ref, ref, sem, target)

    def start(self):
        block = self.here()
        for d, s in NEAR:
            self.push(block, None, self.device(self.first + s, self.second), self.near_sem.at[d])
        self.across(0)

    def across(self, k):
        block = self.slot(self.first + ORDER[k], self.second)
        for d, s in NEAR:
            target = self.device(self.first, self.second + s)
            self.push(block, None, target, self.row_sem.at[d, k])

    def relay_near(self):
        for d, s in NEAR:
            block = self.slot(self.first - s, self.second)
            landed(self.piece(block, None), self.near_sem.at[d])
            self.push(block, d, self.device(self.first + s, self.second), self.far_sem.at[d])
            self.across(1 + d)

    def relay_far(self):
        block = self.slot(self.first + 2, self.second)
        for d in (0, 1):
            landed(self.piece(block, d), self.far_sem.at[d])
        self.across(3)

    def relay_row(self, k):
        for d, s in NEAR:
            block = self.slot(self.first + ORDER[k], self.second - s)
            landed(self.piece(block, None), self.row_sem.at[d, k])
            target = self.device(self.first, self.second + s)
            self.push(block, d, target, self.row_far_sem.at[d, k])

    def end_row(self, k):
        block = self.slot(self.first + ORDER[k], self.second + 2)
        for d in (0, 1):
            landed(self.piece(block, d), self.row_far_sem.at[d, k])


class Scatter(Ring):
    def __init__(self, x_first, parts, via, near, part, via_last, near_last, send_sem, *sems):
        super().__init__(x_first)
        self.parts, self.via, self.near, self.part = parts, via, near, part
        self.via_last, self.near_last = via_last, near_last
        self.send_sem = send_sem
        self.via_sem, self.near_sem, self.via_last_sem, self.near_last_sem = sems
        self.half = parts.shape[1] // 2

    def rows(self, half):
        return pl.ds(half * self.half, self.half)

    def block(self, step, i):
        return self.slot(self.first + step, self.second + LEAVE[i])

    def send_far(self, i):
        block = self.block(2, i)
        for d, s in NEAR:
            target = self.device(self.first + s, self.second)
            src = self.parts.at[block, self.rows(1 - d)]
            self.send(src, self.via.at[d, i], self.via_sem.at[d, i], target)

    def send_near(self, d, i):
        s = NEAR[d][1]
        block = self.block(s, i)
        landed(self.via.at[d, i], self.via_sem.at[d, i])
        rows = self.rows(1 - d)
        mine = self.parts[block, rows].astype(F32)
        self.parts[block, rows] = (mine + self.via[d, i].astype(F32)).astype(BF16)
        target = self.device(self.first + s, self.second)
        self.send(self.parts.at[block], self.near.at[d, i], self.near_sem.at[d, i], target)

    def total(self, i):
        for d in (0, 1):
            landed(self.near.at[d, i], self.near_sem.at[d, i])
        mine = self.parts[self.block(0, i)].astype(F32)
        return mine + self.near[0, i].astype(F32) + self.near[1, i].astype(F32)

    def keep(self, i):
        self.part[i] = self.total(i).astype(BF16)

    def send_far_last(self):
        for d, s in NEAR:
            target = self.device(self.first, self.second + s)
            src = self.part.at[0, self.rows(1 - d)]
            self.send(src, self.via_last.at[d], self.via_last_sem.at[d], target)

    def send_near_last(self, d):
        landed(self.via_last.at[d], self.via_last_sem.at[d])
        rows = self.rows(1 - d)
        mine = self.part[1 + d, rows].astype(F32)
        self.part[1 + d, rows] = (mine + self.via_last[d].astype(F32)).astype(BF16)
        target = self.device(self.first, self.second + NEAR[d][1])
        self.send(self.part.at[1 + d], self.near_last.at[d], self.near_last_sem.at[d], target)

    def last(self, out_ref):
        for d in (0, 1):
            landed(self.near_last.at[d], self.near_last_sem.at[d])
        mine = self.total(3)
        out_ref[...] = mine + self.near_last[0].astype(F32) + self.near_last[1].astype(F32)


class Exchange:
    def __init__(self, count, send, recv, send_sem, recv_sem):
        self.count = count
        self.send, self.recv = send, recv
        self.send_sem, self.recv_sem = send_sem, recv_sem
        self.ep, self.rep = lax.axis_index("ep"), lax.axis_index("rep")

    def copy(self, other, place):
        return pltpu.make_async_remote_copy(
            src_ref=self.send.at[other],
            dst_ref=self.recv.at[place],
            send_sem=self.send_sem.at[0],
            recv_sem=self.recv_sem.at[0],
            device_id=(other, self.rep),
            device_id_type=MESH,
        )

    def each(self, body):
        def run(i, carry):
            body(lax.rem(self.ep + i, self.count))
            return carry

        lax.fori_loop(1, self.count, run, 0)

    def start(self):
        self.each(lambda other: self.copy(other, self.ep).start())
        self.recv[self.ep] = self.send[self.ep]

    def arrive(self):
        landed(self.recv.at[pl.ds(0, self.count - 1)], self.recv_sem.at[0])

    def finish(self):
        landed(self.send.at[pl.ds(0, self.count - 1)], self.send_sem.at[0])


def announce(count):
    ep, rep = lax.axis_index("ep"), lax.axis_index("rep")
    barrier = pltpu.get_barrier_semaphore()

    def run(i, carry):
        other = lax.rem(ep + i, count)
        pl.semaphore_signal(barrier, inc=1, device_id=(other, rep), device_id_type=MESH)
        return carry

    lax.fori_loop(1, count, run, 0)
    ring = Ring(True)
    for _, s in NEAR:
        for target in (ring.device(ring.first + s, ring.second), ring.device(ring.first, ring.second + s)):
            pl.semaphore_signal(barrier, inc=1, device_id=(ep, target), device_id_type=MESH)


def enter(count):
    pl.semaphore_wait(pltpu.get_barrier_semaphore(), count - 1 + 4)


def unpack(packed_ref, rows_ref):
    count, _, half = packed_ref.shape
    step = 4

    def run(i, carry):
        block = packed_ref[pl.ds(i * step, step)].astype(F32)
        at = pl.ds(pl.multiple_of(i * step * CAP, step * CAP), step * CAP)
        rows_ref[at, :half] = block[:, :CAP].reshape(step * CAP, half).astype(BF16)
        rows_ref[at, half:] = block[:, CAP:].reshape(step * CAP, half).astype(BF16)
        return carry

    lax.fori_loop(0, count // step, run, 0)


def pack(rows_ref, packed_ref):
    count, _, half = packed_ref.shape
    step = 4

    def run(i, carry):
        block = rows_ref[pl.ds(pl.multiple_of(i * step * CAP, step * CAP), step * CAP)]
        block = block.reshape(step, CAP, 2 * half)
        both = jnp.concatenate([block[:, :, :half], block[:, :, half:]], axis=1)
        packed_ref[pl.ds(i * step, step)] = both.astype(BF16)
        return carry

    lax.fori_loop(0, count // step, run, 0)


def weight_rows(weight_ref, j):
    pair = weight_ref[pl.ds(2 * j, 2)]
    return pair.reshape(2 * pair.shape[1], pair.shape[2])


def hidden_grads(slopes_in_ref, down_ref, wide_ref, side):
    unit = down_ref.shape[1]

    def run(i, carry):
        j = (SIDE // 2) * i + side
        grads = contract_last(slopes_in_ref[...], weight_rows(down_ref, j))
        wide_ref[2 * j] = grads[:, :unit]
        wide_ref[2 * j + 1] = grads[:, unit:]
        return carry

    lax.fori_loop(0, SIDE, run, 0, unroll=True)


def hidden_units(rows_ref, up_ref, wide_ref, hidden_ref, slopes_ref):
    unit = up_ref.shape[1]

    def run(j, carry):
        both = contract_last(rows_ref[...], weight_rows(up_ref, j))
        for i in range(2):
            pre = both[:, i * unit : (i + 1) * unit]
            slot = 2 * j + i
            other = lax.rem(slot, SIDE) * SIDE + lax.div(slot, SIDE)
            part = 0.5 * jnp.tanh(0.5 * pre) + 0.5
            value = pre * part
            slopes = wide_ref[other] * (part + value * (1.0 - part))
            at = pl.ds(pl.multiple_of(other * unit, unit), unit)
            hidden_ref[:, at] = value.astype(BF16)
            at = pl.ds(pl.multiple_of(slot * unit, unit), unit)
            slopes_ref[:, at] = slopes.astype(BF16)
        return carry

    lax.fori_loop(0, up_ref.shape[0] // 2, run, 0, unroll=True)


def project(left_ref, weight_ref, sum_ref):
    tile = 256

    def run(j, carry):
        at = pl.ds(pl.multiple_of(j * tile, tile), tile)
        right = weight_ref[:, :, at].reshape(-1, tile)
        sum_ref[:, at] = jnp.dot(left_ref[...], right, preferred_element_type=F32)
        return carry

    lax.fori_loop(0, sum_ref.shape[1] // tile, run, 0, unroll=True)


def weight_grads(scatter, step, left_ref, right_ref):
    unit = scatter.parts.shape[1]
    first = scatter.slot(scatter.first + step, 0)

    def run(i, carry):
        block = first + 2 * i
        left = left_ref[:, pl.ds(pl.multiple_of(block * unit, 2 * unit), 2 * unit)]
        grads = contract_first(left, right_ref[...]).astype(BF16)
        scatter.parts[pl.ds(block, 2)] = grads.reshape(2, unit, -1)
        return carry

    lax.fori_loop(0, SIDE // 2, run, 0, unroll=True)


def block_kernel(count, *refs):
    names = iter(refs)

    def take(n):
        return [next(names) for _ in range(n)]

    inputs = take(8)
    block_out, frame_grad, up_grad, down_grad = take(4)
    up_all, down_all = take(2)
    length, routes, gates, frames, kernel, cot = take(6)
    ranks, place, turned, mask, gate = take(5)
    normed, hat1, inv1, pad, conv, res, hat2, inv2 = take(8)
    send_slopes, send_rows, recv_slopes, recv_rows = take(4)
    back_out, back_grad, recv_out, recv_grad = take(4)
    slopes_in, rows_in, wide, hidden, slopes, row_sum = take(6)
    normed_grad, first_grad = take(2)
    up_parts, down_parts = take(2)
    up_room, down_room = take(5), take(5)
    (in_sem,) = take(1)
    exchange_sems = [take(2) for _ in range(4)]
    gather_sems = [take(5) for _ in range(2)]
    scatter_sems = [take(5) for _ in range(2)]

    gathers = [Gather(True, up_all, *gather_sems[0]), Gather(False, down_all, *gather_sems[1])]
    homes = (length, routes, gates, frames, kernel)
    homes += (up_all.at[gathers[0].here()], down_all.at[gathers[1].here()], cot)
    own = [pltpu.make_async_copy(a, b, in_sem.at[i]) for i, (a, b) in enumerate(zip(inputs, homes))]
    announce(count)
    for i in (1, 0, 2, 7, 5, 6, 3, 4):
        own[i].start()

    to_slopes = Exchange(count, send_slopes, recv_slopes, *exchange_sems[0])
    to_rows = Exchange(count, send_rows, recv_rows, *exchange_sems[1])
    to_out = Exchange(count, back_out, recv_out, *exchange_sems[2])
    to_grad = Exchange(count, back_grad, recv_grad, *exchange_sems[3])
    scatters = [
        Scatter(True, up_parts, *up_room, *scatter_sems[0]),
        Scatter(False, down_parts, *down_room, *scatter_sems[1]),
    ]
    sides = [(slopes, rows_in), (hidden, slopes_in)]

    own[1].wait()
    route_places(routes, ranks, place)
    own[0].wait()
    own[2].wait()
    live_columns(length, gates, mask, gate)
    own[7].wait()
    pack_slopes(cot, gate, place, send_slopes)
    enter(count)
    to_slopes.start()
    for i in (5, 6):
        own[i].wait()
    for gather in gathers:
        gather.start()
    for i in (3, 4):
        own[i].wait()
    front_norm(frames, mask, hat1, inv1, pad)
    depthwise(pad, kernel, conv, False)
    front_residual(frames, conv, res, hat2, inv2, normed)
    pack_rows(normed, place, send_rows)
    to_rows.start()

    for gather in gathers:
        gather.relay_near()
    for gather in gathers:
        gather.relay_row(0)
    for gather in gathers:
        gather.relay_far()
    for k in (1, 2, 3):
        for gather in gathers:
            gather.relay_row(k)
    turn_places(ranks, turned)
    to_slopes.arrive()
    unpack(recv_slopes, slopes_in)
    near_side = lax.div(gathers[1].second, SIDE // 2)
    hidden_grads(slopes_in, down_all, wide, near_side)
    for k in range(SIDE):
        for gather in gathers:
            gather.end_row(k)
    hidden_grads(slopes_in, down_all, wide, 1 - near_side)
    to_rows.arrive()
    unpack(recv_rows, rows_in)
    hidden_units(rows_in, up_all, wide, hidden, slopes)
    project(slopes, up_all, row_sum)
    pack(row_sum, back_grad)
    to_grad.start()

    def each(step):
        for scatter in scatters:
            step(scatter)

    def both_near(i):
        for d in (0, 1):
            each(lambda scatter: scatter.send_near(d, i))

    def all_grads(step):
        for scatter, (left, right) in zip(scatters, sides):
            weight_grads(scatter, step, left, right)

    all_grads(2)
    each(lambda scatter: scatter.send_far(0))
    each(lambda scatter: scatter.send_far(1))
    project(hidden, down_all, row_sum)
    pack(row_sum, back_out)
    to_out.start()
    all_grads(1)
    all_grads(-1)
    each(lambda scatter: scatter.send_far(2))
    both_near(0)
    each(lambda scatter: scatter.send_far(3))
    both_near(1)
    all_grads(0)
    both_near(2)
    each(lambda scatter: scatter.keep(0))
    each(lambda scatter: scatter.send_far_last())
    both_near(3)
    for d in (0, 1):
        each(lambda scatter: scatter.keep(1 + d))
        each(lambda scatter: scatter.send_near_last(d))

    to_grad.arrive()
    back_slopes(recv_grad, turned, normed_grad)
    back_residual(cot, hat2, inv2, conv, normed_grad, pad)
    depthwise(pad, kernel, first_grad, True)
    back_frames(first_grad, mask, hat1, inv1, normed_grad, frame_grad)
    for scatter, out in zip(scatters, (up_grad, down_grad)):
        scatter.last(out)
    to_out.arrive()
    back_mix(recv_out, turned, gate, res, block_out)

    for exchange in (to_slopes, to_rows, to_out, to_grad):
        exchange.finish()
    for ring, blocks in zip(gathers + scatters, (up_all, down_all, up_parts, down_parts)):
        ring.finish(blocks)


def hand_over(*refs):
    n = (len(refs) - 1) // 2
    copies = [pltpu.make_async_copy(refs[i], refs[n + i], refs[-1].at[i]) for i in range(n)]
    for copy in copies:
        copy.start()
    for copy in copies:
        copy.wait()


def on_device(frames, lengths, routes, gate_weights, kernel, up_weight, down_weight, cotangent):
    experts = lax.axis_size("ep")
    reps = lax.axis_size("rep")
    count, width = frames.shape
    unit = up_weight.shape[1]
    rows = experts * CAP
    half = width // 2
    vmem = pltpu.VMEM
    packed = vmem((experts, 2 * CAP, half), BF16)
    grid32 = vmem((count, width), F32)
    column = vmem((count, 1), F32)
    weights = vmem((reps, unit, width), BF16)
    room = [
        vmem((2, SIDE, unit // 2, width), BF16),
        vmem((2, SIDE, unit, width), BF16),
        vmem((3, unit, width), BF16),
        vmem((2, unit // 2, width), BF16),
        vmem((2, unit, width), BF16),
    ]
    narrow = vmem((count, width), BF16)
    scratch = [weights, weights]
    scratch += [vmem((1, 1), jnp.int32), vmem((2, count), jnp.int32), vmem((2, count), F32)]
    scratch += [narrow, vmem(kernel.shape, F32), narrow]
    scratch += [vmem((2, count), F32), vmem((2 * rows, 4 * count), BF16)]
    scratch += [vmem((4, count, 2 * rows), BF16), column, vmem((2, count, 1), F32)]
    scratch += [narrow, grid32, column, vmem((count + 2 * EDGE, width), F32)]
    scratch += [grid32, grid32, grid32, column]
    scratch += [packed] * 8
    scratch += [vmem((rows, width), BF16)] * 2
    scratch += [vmem((reps, rows, unit), F32)]
    scratch += [vmem((rows, reps * unit), BF16)] * 2
    scratch += [vmem((rows, width), F32)]
    scratch += [grid32, grid32, weights, weights] + room + room
    scratch += [DMA((8,))]
    scratch += [DMA((1,))] * 8
    scratch += [DMA((1,)), DMA((2,)), DMA((2,)), DMA((2, SIDE)), DMA((2, SIDE))] * 2
    scratch += [DMA((1,)), DMA((2, SIDE)), DMA((2, SIDE)), DMA((2,)), DMA((2,))] * 2

    anywhere = pl.BlockSpec(memory_space=pl.ANY)
    in_vmem = pl.BlockSpec(memory_space=pltpu.VMEM)
    shapes = [jax.ShapeDtypeStruct((count, width), BF16)] * 2
    shapes += [jax.ShapeDtypeStruct((unit, width), F32)] * 2
    results = pl.pallas_call(
        functools.partial(block_kernel, experts),
        out_shape=[vmem(s.shape, s.dtype) for s in shapes],
        in_specs=[anywhere] * 8,
        out_specs=[in_vmem] * 4,
        scratch_shapes=scratch,
        compiler_params=pltpu.CompilerParams(
            collective_id=0, has_side_effects=True, vmem_limit_bytes=58 << 20
        ),
        cost_estimate=pl.CostEstimate(
            flops=12 * rows * reps * unit * width, bytes_accessed=8 << 20, transcendentals=0
        ),
    )(
        lengths.reshape(1, 1),
        routes.T,
        gate_weights.T,
        frames,
        kernel,
        up_weight[0],
        down_weight[0],
        cotangent,
    )
    block_out, frame_grad, up_grad, down_grad = pl.pallas_call(
        hand_over,
        out_shape=shapes,
        in_specs=[anywhere] * 4,
        out_specs=[anywhere] * 4,
        scratch_shapes=[DMA((4,))],
        compiler_params=pltpu.CompilerParams(vmem_limit_bytes=4 << 20),
    )(*results)
    return block_out, frame_grad, up_grad[None], down_grad[None]


def solution(mesh):
    in_specs = (
        P(("ep", "rep"), None),
        P(("ep", "rep")),
        P(("ep", "rep"), None),
        P(("ep", "rep"), None),
        P(),
        P("ep", "rep", None),
        P("ep", "rep", None),
        P(("ep", "rep"), None),
    )
    out_specs = (
        P(("ep", "rep"), None),
        P(("ep", "rep"), None),
        P("ep", "rep", None),
        P("ep", "rep", None),
    )
    return jax.shard_map(
        on_device, mesh=mesh, in_specs=in_specs, out_specs=out_specs, check_vma=False
    )
```

```python
import functools

import jax
import jax.numpy as jnp
from jax import lax
from jax.experimental import pallas as pl
from jax.experimental.pallas import tpu as pltpu
from jax.sharding import PartitionSpec as P

MESH = pl.DeviceIdType.MESH
DMA = pltpu.SemaphoreType.DMA
F32 = jnp.float32
BF16 = jnp.bfloat16

EPS = 1e-05
SIDE = 4
CAP = 8
TAPS = 31
EDGE = 16
NEAR = ((0, 1), (1, -1))
ORDER = (0, -1, 1, 2)
LEAVE = (2, 1, -1, 0)


def wrap(i, n):
    return lax.rem(i + n, n)


def lane_iota(shape):
    return lax.broadcasted_iota(jnp.int32, shape, 1)


def landed(ref, sem):
    pltpu.make_async_copy(ref, ref, sem).wait()


def to_column(row):
    count = row.shape[1]
    square = (count, count)
    here = lane_iota(square) == lax.broadcasted_iota(jnp.int32, square, 0)
    return jnp.sum(jnp.where(here, row, 0.0), axis=1, keepdims=True)


def route_places(routes_ref, rank_ref, place_ref):
    experts = place_ref.shape[0] // (2 * CAP)
    count = routes_ref.shape[1]
    shape = (experts, count)
    sub = lax.broadcasted_iota(jnp.int32, shape, 0)
    hot = [sub == routes_ref[k : k + 1] for k in range(2)]
    both = (hot[0].astype(F32) + hot[1].astype(F32)).astype(BF16)
    square = (count, count)
    earlier = lax.broadcasted_iota(jnp.int32, square, 0) < lane_iota(square)
    before = jnp.dot(both, earlier.astype(F32).astype(BF16), preferred_element_type=F32)
    tall = lax.broadcasted_iota(jnp.int32, (place_ref.shape[0], count), 0).astype(F32)
    for k in range(2):
        rank = jnp.sum(jnp.where(hot[k], before, 0.0), axis=0, keepdims=True)
        row = routes_ref[k : k + 1].astype(F32) * (2 * CAP) + rank
        rank_ref[k : k + 1] = row
        for h in range(2):
            at = slice((2 * k + h) * count, (2 * k + h + 1) * count)
            place_ref[:, at] = (tall == row + h * CAP).astype(F32).astype(BF16)


def turn_places(rank_ref, turned_ref):
    _, count, width = turned_ref.shape
    wide = lane_iota((count, width)).astype(F32)
    for k in range(2):
        row = to_column(rank_ref[k : k + 1])
        for h in range(2):
            turned_ref[2 * k + h] = (wide == row + h * CAP).astype(F32).astype(BF16)


def live_columns(length_ref, gates_ref, mask_ref, gate_ref):
    count = mask_ref.shape[0]
    positions = lax.broadcasted_iota(jnp.int32, (count, 1), 0)
    mask = (positions < length_ref[...]).astype(F32)
    mask_ref[...] = mask
    for k in range(2):
        gate_ref[k] = to_column(gates_ref[k : k + 1]) * mask


def contract_first(left, right):
    return lax.dot_general(left, right, (((0,), (0,)), ((), ())), preferred_element_type=F32)


def contract_last(left, right):
    return lax.dot_general(left, right, (((1,), (1,)), ((), ())), preferred_element_type=F32)


def pack_slopes(cot_ref, gate_ref, place_ref, out_ref):
    width = cot_ref.shape[1]
    half = width // 2
    cot = cot_ref[...].astype(F32)
    parts = []
    for k in range(2):
        scaled = (gate_ref[k] * cot).astype(BF16)
        parts += [scaled[:, :half], scaled[:, half:]]
    stacked = jnp.concatenate(parts, axis=0)
    packed = jnp.dot(place_ref[...], stacked, preferred_element_type=F32)
    out_ref[...] = packed.astype(BF16).reshape(out_ref.shape)


def pack_rows(normed_ref, place_ref, out_ref):
    width = normed_ref.shape[1]
    half = width // 2
    stacked = jnp.concatenate([normed_ref[:, :half], normed_ref[:, half:]], axis=0)
    middle = place_ref.shape[1] // 2
    place = place_ref[:, :middle] + place_ref[:, middle:]
    packed = jnp.dot(place, stacked, preferred_element_type=F32)
    out_ref[...] = packed.astype(BF16).reshape(out_ref.shape)


def over_rows(count, step, body):
    def run(i, carry):
        body(pl.ds(pl.multiple_of(i * step, step), step), pl.multiple_of(i * step, step))
        return carry

    lax.fori_loop(0, count // step, run, 0)


def normalize(values):
    center = values - jnp.mean(values, axis=-1, keepdims=True)
    inverse = lax.rsqrt(jnp.mean(center * center, axis=-1, keepdims=True) + EPS)
    return center * inverse, inverse


def norm_back(normed, inverse, upstream):
    mean_grad = jnp.mean(upstream, axis=-1, keepdims=True)
    mean_cross = jnp.mean(upstream * normed, axis=-1, keepdims=True)
    return inverse * (upstream - mean_grad - normed * mean_cross)


def silu_slope(values):
    part = jax.nn.sigmoid(values)
    return part + values * part * (1.0 - part)


def depthwise(pad_ref, kernel_ref, out_ref, reverse):
    count, width = out_ref.shape
    columns = 128

    def run(i, carry):
        at = pl.ds(pl.multiple_of(i * columns, columns), columns)
        total = jnp.zeros((count, columns), F32)
        for shift in range(8):
            part = None
            for base in range(0, 32, 8):
                j = base + shift - 1
                if j < 0 or j >= TAPS:
                    continue
                row = TAPS - 1 - j if reverse else j
                term = kernel_ref[row : row + 1, at] * pad_ref[base : base + count + 8, at]
                part = term if part is None else part + term
            if shift:
                part = pltpu.roll(part, count + 8 - shift, 0)
            total = total + part[:count]
        out_ref[:, at] = total
        return carry

    lax.fori_loop(0, width // columns, run, 0)


def front_norm(frames_ref, mask_ref, hat_ref, inv_ref, pad_ref):
    count, width = frames_ref.shape
    pad_ref[:EDGE] = jnp.zeros((EDGE, width), F32)
    pad_ref[EDGE + count :] = jnp.zeros((EDGE, width), F32)

    def body(at, start):
        hat, inverse = normalize(frames_ref[at].astype(F32))
        hat_ref[at] = hat
        inv_ref[at] = inverse
        pad_ref[pl.ds(start + EDGE, 16)] = hat * mask_ref[at]

    over_rows(count, 16, body)


def front_residual(frames_ref, conv_ref, res_ref, hat_ref, inv_ref, normed_ref):
    def body(at, start):
        residual = frames_ref[at].astype(F32) + jax.nn.silu(conv_ref[at])
        hat, inverse = normalize(residual)
        res_ref[at] = residual
        hat_ref[at] = hat
        inv_ref[at] = inverse
        normed_ref[at] = hat.astype(BF16)

    over_rows(frames_ref.shape[0], 16, body)


def back_mix(back_ref, place_ref, gate_ref, res_ref, out_ref):
    half = back_ref.shape[2]
    rows = back_ref[...].reshape(-1, half)
    for h in range(2):
        at = slice(h * half, (h + 1) * half)
        mixed = gate_ref[0] * jnp.dot(place_ref[h], rows, preferred_element_type=F32)
        mixed += gate_ref[1] * jnp.dot(place_ref[2 + h], rows, preferred_element_type=F32)
        out_ref[:, at] = (res_ref[:, at] + mixed).astype(BF16)


def back_slopes(back_ref, place_ref, grad_ref):
    half = back_ref.shape[2]
    rows = back_ref[...].reshape(-1, half)
    for h in range(2):
        pick = place_ref[h] + place_ref[2 + h]
        grad_ref[:, h * half : (h + 1) * half] = jnp.dot(pick, rows, preferred_element_type=F32)


def back_residual(cot_ref, hat_ref, inv_ref, conv_ref, grad_ref, pad_ref):
    def body(at, start):
        grad = cot_ref[at].astype(F32) + norm_back(hat_ref[at], inv_ref[at], grad_ref[at])
        grad_ref[at] = grad
        pad_ref[pl.ds(start + EDGE, 16)] = grad * silu_slope(conv_ref[at])

    over_rows(cot_ref.shape[0], 16, body)


def back_frames(first_ref, mask_ref, hat_ref, inv_ref, grad_ref, out_ref):
    def body(at, start):
        first = first_ref[at] * mask_ref[at]
        out_ref[at] = (grad_ref[at] + norm_back(hat_ref[at], inv_ref[at], first)).astype(BF16)

    over_rows(out_ref.shape[0], 16, body)


class Ring:
    def __init__(self, x_first):
        rep = lax.axis_index("rep")
        x, y = lax.rem(rep, SIDE), lax.div(rep, SIDE)
        self.x_first = x_first
        self.ep = lax.axis_index("ep")
        self.first, self.second = (x, y) if x_first else (y, x)

    def device(self, first, second):
        first, second = wrap(first, SIDE), wrap(second, SIDE)
        return second * SIDE + first if self.x_first else first * SIDE + second

    def here(self):
        return self.slot(self.first, self.second)

    def slot(self, first, second):
        return wrap(first, SIDE) * SIDE + wrap(second, SIDE)

    def send(self, src, dst, recv_sem, target):
        pltpu.make_async_remote_copy(
            src_ref=src,
            dst_ref=dst,
            send_sem=self.send_sem.at[0],
            recv_sem=recv_sem,
            device_id=(self.ep, target),
            device_id_type=MESH,
        ).start()

    def finish(self, blocks):
        landed(blocks.at[pl.ds(0, SIDE * SIDE - 1)], self.send_sem.at[0])


class Gather(Ring):
    def __init__(self, x_first, full, send_sem, near_sem, far_sem, row_sem, row_far_sem):
        super().__init__(x_first)
        self.full, self.send_sem = full, send_sem
        self.near_sem, self.far_sem = near_sem, far_sem
        self.row_sem, self.row_far_sem = row_sem, row_far_sem
        self.half = full.shape[1] // 2

    def piece(self, block, half):
        if half is None:
            return self.full.at[block]
        return self.full.at[block, pl.ds(half * self.half, self.half)]

    def push(self, block, half, target, sem):
        ref = self.piece(block, half)
        self.send(ref, ref, sem, target)

    def start(self):
        block = self.here()
        for d, s in NEAR:
            self.push(block, None, self.device(self.first + s, self.second), self.near_sem.at[d])
        self.across(0)

    def across(self, k):
        block = self.slot(self.first + ORDER[k], self.second)
        for d, s in NEAR:
            target = self.device(self.first, self.second + s)
            self.push(block, None, target, self.row_sem.at[d, k])

    def relay_near(self):
        for d, s in NEAR:
            block = self.slot(self.first - s, self.second)
            landed(self.piece(block, None), self.near_sem.at[d])
            self.push(block, d, self.device(self.first + s, self.second), self.far_sem.at[d])
            self.across(1 + d)

    def relay_far(self):
        block = self.slot(self.first + 2, self.second)
        for d in (0, 1):
            landed(self.piece(block, d), self.far_sem.at[d])
        self.across(3)

    def relay_row(self, k):
        for d, s in NEAR:
            block = self.slot(self.first + ORDER[k], self.second - s)
            landed(self.piece(block, None), self.row_sem.at[d, k])
            target = self.device(self.first, self.second + s)
            self.push(block, d, target, self.row_far_sem.at[d, k])

    def end_row(self, k):
        block = self.slot(self.first + ORDER[k], self.second + 2)
        for d in (0, 1):
            landed(self.piece(block, d), self.row_far_sem.at[d, k])


class Scatter(Ring):
    def __init__(self, x_first, parts, via, near, part, via_last, near_last, send_sem, *sems):
        super().__init__(x_first)
        self.parts, self.via, self.near, self.part = parts, via, near, part
        self.via_last, self.near_last = via_last, near_last
        self.send_sem = send_sem
        self.via_sem, self.near_sem, self.via_last_sem, self.near_last_sem = sems
        self.half = parts.shape[1] // 2

    def rows(self, half):
        return pl.ds(half * self.half, self.half)

    def block(self, step, i):
        return self.slot(self.first + step, self.second + LEAVE[i])

    def send_far(self, i):
        block = self.block(2, i)
        for d, s in NEAR:
            target = self.device(self.first + s, self.second)
            src = self.parts.at[block, self.rows(1 - d)]
            self.send(src, self.via.at[d, i], self.via_sem.at[d, i], target)

    def send_near(self, d, i):
        s = NEAR[d][1]
        block = self.block(s, i)
        landed(self.via.at[d, i], self.via_sem.at[d, i])
        rows = self.rows(1 - d)
        mine = self.parts[block, rows].astype(F32)
        self.parts[block, rows] = (mine + self.via[d, i].astype(F32)).astype(BF16)
        target = self.device(self.first + s, self.second)
        self.send(self.parts.at[block], self.near.at[d, i], self.near_sem.at[d, i], target)

    def total(self, i):
        for d in (0, 1):
            landed(self.near.at[d, i], self.near_sem.at[d, i])
        mine = self.parts[self.block(0, i)].astype(F32)
        return mine + self.near[0, i].astype(F32) + self.near[1, i].astype(F32)

    def keep(self, i):
        self.part[i] = self.total(i).astype(BF16)

    def send_far_last(self):
        for d, s in NEAR:
            target = self.device(self.first, self.second + s)
            src = self.part.at[0, self.rows(1 - d)]
            self.send(src, self.via_last.at[d], self.via_last_sem.at[d], target)

    def send_near_last(self, d):
        landed(self.via_last.at[d], self.via_last_sem.at[d])
        rows = self.rows(1 - d)
        mine = self.part[1 + d, rows].astype(F32)
        self.part[1 + d, rows] = (mine + self.via_last[d].astype(F32)).astype(BF16)
        target = self.device(self.first, self.second + NEAR[d][1])
        self.send(self.part.at[1 + d], self.near_last.at[d], self.near_last_sem.at[d], target)

    def last(self, out_ref):
        for d in (0, 1):
            landed(self.near_last.at[d], self.near_last_sem.at[d])
        mine = self.total(3)
        out_ref[...] = mine + self.near_last[0].astype(F32) + self.near_last[1].astype(F32)


class Exchange:
    def __init__(self, count, send, recv, send_sem, recv_sem):
        self.count = count
        self.send, self.recv = send, recv
        self.send_sem, self.recv_sem = send_sem, recv_sem
        self.ep, self.rep = lax.axis_index("ep"), lax.axis_index("rep")

    def copy(self, other, place):
        return pltpu.make_async_remote_copy(
            src_ref=self.send.at[other],
            dst_ref=self.recv.at[place],
            send_sem=self.send_sem.at[0],
            recv_sem=self.recv_sem.at[0],
            device_id=(other, self.rep),
            device_id_type=MESH,
        )

    def each(self, body):
        def run(i, carry):
            body(lax.rem(self.ep + i, self.count))
            return carry

        lax.fori_loop(1, self.count, run, 0)

    def start(self):
        self.each(lambda other: self.copy(other, self.ep).start())
        self.recv[self.ep] = self.send[self.ep]

    def arrive(self):
        landed(self.recv.at[pl.ds(0, self.count - 1)], self.recv_sem.at[0])

    def finish(self):
        landed(self.send.at[pl.ds(0, self.count - 1)], self.send_sem.at[0])


def announce(count):
    ep, rep = lax.axis_index("ep"), lax.axis_index("rep")
    barrier = pltpu.get_barrier_semaphore()

    def run(i, carry):
        other = lax.rem(ep + i, count)
        pl.semaphore_signal(barrier, inc=1, device_id=(other, rep), device_id_type=MESH)
        return carry

    lax.fori_loop(1, count, run, 0)
    ring = Ring(True)
    for _, s in NEAR:
        for target in (ring.device(ring.first + s, ring.second), ring.device(ring.first, ring.second + s)):
            pl.semaphore_signal(barrier, inc=1, device_id=(ep, target), device_id_type=MESH)


def enter(count):
    pl.semaphore_wait(pltpu.get_barrier_semaphore(), count - 1 + 4)


def unpack(packed_ref, rows_ref):
    count, _, half = packed_ref.shape
    step = 4

    def run(i, carry):
        block = packed_ref[pl.ds(i * step, step)].astype(F32)
        at = pl.ds(pl.multiple_of(i * step * CAP, step * CAP), step * CAP)
        rows_ref[at, :half] = block[:, :CAP].reshape(step * CAP, half).astype(BF16)
        rows_ref[at, half:] = block[:, CAP:].reshape(step * CAP, half).astype(BF16)
        return carry

    lax.fori_loop(0, count // step, run, 0)


def weight_rows(weight_ref, j):
    pair = weight_ref[pl.ds(2 * j, 2)]
    return pair.reshape(2 * pair.shape[1], pair.shape[2])


def hidden_grads(slopes_in_ref, down_ref, wide_ref, side):
    unit = down_ref.shape[1]

    def run(i, carry):
        j = (SIDE // 2) * i + side
        grads = contract_last(slopes_in_ref[...], weight_rows(down_ref, j))
        wide_ref[2 * j] = grads[:, :unit]
        wide_ref[2 * j + 1] = grads[:, unit:]
        return carry

    lax.fori_loop(0, SIDE, run, 0, unroll=True)


def hidden_units(rows_ref, up_ref, wide_ref, hidden_ref, slopes_ref):
    unit = up_ref.shape[1]

    def run(j, carry):
        both = contract_last(rows_ref[...], weight_rows(up_ref, j))
        for i in range(2):
            pre = both[:, i * unit : (i + 1) * unit]
            slot = 2 * j + i
            other = lax.rem(slot, SIDE) * SIDE + lax.div(slot, SIDE)
            part = 0.5 * jnp.tanh(0.5 * pre) + 0.5
            value = pre * part
            slopes = wide_ref[other] * (part + value * (1.0 - part))
            at = pl.ds(pl.multiple_of(other * unit, unit), unit)
            hidden_ref[:, at] = value.astype(BF16)
            at = pl.ds(pl.multiple_of(slot * unit, unit), unit)
            slopes_ref[:, at] = slopes.astype(BF16)
        return carry

    lax.fori_loop(0, up_ref.shape[0] // 2, run, 0, unroll=True)


def project(left_ref, weight_ref, packed_ref):
    count, _, half = packed_ref.shape
    tile = 256

    def run(j, carry):
        parts = []
        for h in range(2):
            at = pl.ds(pl.multiple_of(h * half + j * tile, tile), tile)
            right = weight_ref[:, :, at].reshape(-1, tile)
            part = jnp.dot(left_ref[...], right, preferred_element_type=F32)
            parts.append(part.reshape(count, CAP, tile))
        at = pl.ds(pl.multiple_of(j * tile, tile), tile)
        packed_ref[:, :, at] = jnp.concatenate(parts, axis=1).astype(BF16)
        return carry

    lax.fori_loop(0, half // tile, run, 0, unroll=True)


def weight_grads(scatter, step, left_ref, right_ref):
    unit = scatter.parts.shape[1]
    first = scatter.slot(scatter.first + step, 0)

    def run(i, carry):
        block = first + 2 * i
        left = left_ref[:, pl.ds(pl.multiple_of(block * unit, 2 * unit), 2 * unit)]
        grads = contract_first(left, right_ref[...]).astype(BF16)
        scatter.parts[pl.ds(block, 2)] = grads.reshape(2, unit, -1)
        return carry

    lax.fori_loop(0, SIDE // 2, run, 0, unroll=True)


def block_kernel(count, *refs):
    names = iter(refs)

    def take(n):
        return [next(names) for _ in range(n)]

    inputs = take(8)
    block_out, frame_grad, up_grad, down_grad = take(4)
    up_all, down_all = take(2)
    length, routes, gates, frames, kernel, cot = take(6)
    ranks, place, turned, mask, gate = take(5)
    normed, hat1, inv1, pad, conv, res, hat2, inv2 = take(8)
    send_slopes, send_rows, recv_slopes, recv_rows = take(4)
    back_out, back_grad, recv_out, recv_grad = take(4)
    slopes_in, rows_in, wide, hidden, slopes = take(5)
    normed_grad, first_grad = take(2)
    up_parts, down_parts = take(2)
    up_room, down_room = take(5), take(5)
    (in_sem,) = take(1)
    exchange_sems = [take(2) for _ in range(4)]
    gather_sems = [take(5) for _ in range(2)]
    scatter_sems = [take(5) for _ in range(2)]

    gathers = [Gather(True, up_all, *gather_sems[0]), Gather(False, down_all, *gather_sems[1])]
    homes = (length, routes, gates, frames, kernel)
    homes += (up_all.at[gathers[0].here()], down_all.at[gathers[1].here()], cot)
    own = [pltpu.make_async_copy(a, b, in_sem.at[i]) for i, (a, b) in enumerate(zip(inputs, homes))]
    announce(count)
    for i in (1, 0, 2, 7, 5, 6, 3, 4):
        own[i].start()

    to_slopes = Exchange(count, send_slopes, recv_slopes, *exchange_sems[0])
    to_rows = Exchange(count, send_rows, recv_rows, *exchange_sems[1])
    to_out = Exchange(count, back_out, recv_out, *exchange_sems[2])
    to_grad = Exchange(count, back_grad, recv_grad, *exchange_sems[3])
    scatters = [
        Scatter(True, up_parts, *up_room, *scatter_sems[0]),
        Scatter(False, down_parts, *down_room, *scatter_sems[1]),
    ]
    sides = [(slopes, rows_in), (hidden, slopes_in)]

    own[1].wait()
    route_places(routes, ranks, place)
    own[0].wait()
    own[2].wait()
    live_columns(length, gates, mask, gate)
    own[7].wait()
    pack_slopes(cot, gate, place, send_slopes)
    enter(count)
    to_slopes.start()
    for i in (5, 6):
        own[i].wait()
    for gather in gathers:
        gather.start()
    for i in (3, 4):
        own[i].wait()
    front_norm(frames, mask, hat1, inv1, pad)
    depthwise(pad, kernel, conv, False)
    front_residual(frames, conv, res, hat2, inv2, normed)
    pack_rows(normed, place, send_rows)
    to_rows.start()

    for gather in gathers:
        gather.relay_near()
    for gather in gathers:
        gather.relay_row(0)
    for gather in gathers:
        gather.relay_far()
    for k in (1, 2, 3):
        for gather in gathers:
            gather.relay_row(k)
    turn_places(ranks, turned)
    to_slopes.arrive()
    unpack(recv_slopes, slopes_in)
    near_side = lax.div(gathers[1].second, SIDE // 2)
    hidden_grads(slopes_in, down_all, wide, near_side)
    for k in range(SIDE):
        for gather in gathers:
            gather.end_row(k)
    hidden_grads(slopes_in, down_all, wide, 1 - near_side)
    to_rows.arrive()
    unpack(recv_rows, rows_in)
    hidden_units(rows_in, up_all, wide, hidden, slopes)
    project(slopes, up_all, back_grad)
    to_grad.start()

    def each(step):
        for scatter in scatters:
            step(scatter)

    def both_near(i):
        for d in (0, 1):
            each(lambda scatter: scatter.send_near(d, i))

    def all_grads(step):
        for scatter, (left, right) in zip(scatters, sides):
            weight_grads(scatter, step, left, right)

    all_grads(2)
    each(lambda scatter: scatter.send_far(0))
    each(lambda scatter: scatter.send_far(1))
    project(hidden, down_all, back_out)
    to_out.start()
    all_grads(1)
    all_grads(-1)
    each(lambda scatter: scatter.send_far(2))
    both_near(0)
    each(lambda scatter: scatter.send_far(3))
    both_near(1)
    all_grads(0)
    both_near(2)
    each(lambda scatter: scatter.keep(0))
    each(lambda scatter: scatter.send_far_last())
    both_near(3)
    for d in (0, 1):
        each(lambda scatter: scatter.keep(1 + d))
        each(lambda scatter: scatter.send_near_last(d))

    to_grad.arrive()
    back_slopes(recv_grad, turned, normed_grad)
    back_residual(cot, hat2, inv2, conv, normed_grad, pad)
    depthwise(pad, kernel, first_grad, True)
    back_frames(first_grad, mask, hat1, inv1, normed_grad, frame_grad)
    for scatter, out in zip(scatters, (up_grad, down_grad)):
        scatter.last(out)
    to_out.arrive()
    back_mix(recv_out, turned, gate, res, block_out)

    for exchange in (to_slopes, to_rows, to_out, to_grad):
        exchange.finish()
    for ring, blocks in zip(gathers + scatters, (up_all, down_all, up_parts, down_parts)):
        ring.finish(blocks)


def hand_over(*refs):
    n = (len(refs) - 1) // 2
    copies = [pltpu.make_async_copy(refs[i], refs[n + i], refs[-1].at[i]) for i in range(n)]
    for copy in copies:
        copy.start()
    for copy in copies:
        copy.wait()


def on_device(frames, lengths, routes, gate_weights, kernel, up_weight, down_weight, cotangent):
    experts = lax.axis_size("ep")
    reps = lax.axis_size("rep")
    count, width = frames.shape
    unit = up_weight.shape[1]
    rows = experts * CAP
    half = width // 2
    vmem = pltpu.VMEM
    packed = vmem((experts, 2 * CAP, half), BF16)
    grid32 = vmem((count, width), F32)
    column = vmem((count, 1), F32)
    weights = vmem((reps, unit, width), BF16)
    room = [
        vmem((2, SIDE, unit // 2, width), BF16),
        vmem((2, SIDE, unit, width), BF16),
        vmem((3, unit, width), BF16),
        vmem((2, unit // 2, width), BF16),
        vmem((2, unit, width), BF16),
    ]
    narrow = vmem((count, width), BF16)
    scratch = [weights, weights]
    scratch += [vmem((1, 1), jnp.int32), vmem((2, count), jnp.int32), vmem((2, count), F32)]
    scratch += [narrow, vmem(kernel.shape, F32), narrow]
    scratch += [vmem((2, count), F32), vmem((2 * rows, 4 * count), BF16)]
    scratch += [vmem((4, count, 2 * rows), BF16), column, vmem((2, count, 1), F32)]
    scratch += [narrow, grid32, column, vmem((count + 2 * EDGE, width), F32)]
    scratch += [grid32, grid32, grid32, column]
    scratch += [packed] * 8
    scratch += [vmem((rows, width), BF16)] * 2
    scratch += [vmem((reps, rows, unit), F32)]
    scratch += [vmem((rows, reps * unit), BF16)] * 2
    scratch += [grid32, grid32, weights, weights] + room + room
    scratch += [DMA((8,))]
    scratch += [DMA((1,))] * 8
    scratch += [DMA((1,)), DMA((2,)), DMA((2,)), DMA((2, SIDE)), DMA((2, SIDE))] * 2
    scratch += [DMA((1,)), DMA((2, SIDE)), DMA((2, SIDE)), DMA((2,)), DMA((2,))] * 2

    anywhere = pl.BlockSpec(memory_space=pl.ANY)
    in_vmem = pl.BlockSpec(memory_space=pltpu.VMEM)
    shapes = [jax.ShapeDtypeStruct((count, width), BF16)] * 2
    shapes += [jax.ShapeDtypeStruct((unit, width), F32)] * 2
    results = pl.pallas_call(
        functools.partial(block_kernel, experts),
        out_shape=[vmem(s.shape, s.dtype) for s in shapes],
        in_specs=[anywhere] * 8,
        out_specs=[in_vmem] * 4,
        scratch_shapes=scratch,
        compiler_params=pltpu.CompilerParams(
            collective_id=0, has_side_effects=True, vmem_limit_bytes=58 << 20
        ),
        cost_estimate=pl.CostEstimate(
            flops=12 * rows * reps * unit * width, bytes_accessed=8 << 20, transcendentals=0
        ),
    )(
        lengths.reshape(1, 1),
        routes.T,
        gate_weights.T,
        frames,
        kernel,
        up_weight[0],
        down_weight[0],
        cotangent,
    )
    block_out, frame_grad, up_grad, down_grad = pl.pallas_call(
        hand_over,
        out_shape=shapes,
        in_specs=[anywhere] * 4,
        out_specs=[anywhere] * 4,
        scratch_shapes=[DMA((4,))],
        compiler_params=pltpu.CompilerParams(vmem_limit_bytes=4 << 20),
    )(*results)
    return block_out, frame_grad, up_grad[None], down_grad[None]


def solution(mesh):
    in_specs = (
        P(("ep", "rep"), None),
        P(("ep", "rep")),
        P(("ep", "rep"), None),
        P(("ep", "rep"), None),
        P(),
        P("ep", "rep", None),
        P("ep", "rep", None),
        P(("ep", "rep"), None),
    )
    out_specs = (
        P(("ep", "rep"), None),
        P(("ep", "rep"), None),
        P("ep", "rep", None),
        P("ep", "rep", None),
    )
    return jax.shard_map(
        on_device, mesh=mesh, in_specs=in_specs, out_specs=out_specs, check_vma=False
    )
```
